256 devices in a mesh: ia: 4 (over x), ja: 8 (over y, core), ka: 8 (over z).
Axes of the slice: x: 4, y: 4, z: 8, core: 2. Of those that a mesh axis runs over, the one named last changes fastest.
Arguments:
- tensor: bfloat16 [64, 2048, 4096], P('ka', 'ia', 'ja'), may hold values from -6 to 6
- factor_b: float32 [32, 4096], P('ia', ('ja', 'ka')), may hold values from -0.09375 to 0.09375
- factor_c: float32 [32, 64], P(('ia', 'ja'), 'ka'), may hold values from -0.75 to 0.75
Outputs:
- factor_a_new: float32 [32, 2048], P('ja', ('ia', 'ka'))
- factor_b_new: float32 [32, 4096], P('ia', ('ja', 'ka'))
The draws below stay inside these ranges and needn't reach their ends.
All inputs are finite; a program needn't handle non-finite values.
Results may differ from the reference program's by a relative error of at most 0.0033.
Values sent between devices are 32-bit elements; how exact they have to be, the bound alone decides.
No kernel may reach another device: no remote copies, remote signals or barrier semaphores. Data moves between devices by JAX's collectives and lax.ppermute only.
A program may use at most 64 MiB of HBM per device.

```python
import jax
import jax.numpy as jnp
from jax import lax

R = 32
I = 2048
J = 4096
K = 64


def block_levels(key, dims, pieces, least, top_value):
    def one(position, parts):
        draws = jax.random.uniform(jax.random.fold_in(jax.random.fold_in(key, 6), position), (parts,), jnp.float32, least / len(pieces), top_value / len(pieces))
        return jnp.repeat(jnp.exp(draws), dims[position] // parts).reshape((-1,) + (1,) * (len(dims) - position - 1))

    level = one(*pieces[0])
    for cut in pieces[1:]:
        level = level * one(*cut)
    return level


def gaussian(stream_key, extent, width, bound, cuts=(), dtype=jnp.bfloat16):
    entries = width * jax.random.normal(stream_key, extent, jnp.float32)
    if cuts:
        entries = entries * block_levels(stream_key, extent, cuts, -0.22, 0.18)
    return jnp.clip(entries, -bound, bound).astype(dtype)


def setup_inputs(seed: int = 0) -> dict:
    arg_keys = jax.random.split(jax.random.key(seed), 4)
    tensor = gaussian(arg_keys[0], (K, I, J), 1.0, 6.0, ((0, 8), (1, 4), (2, 8)))
    factor_b = gaussian(arg_keys[1], (R, J), J ** -0.5, 0.09375, ((0, 4), (1, 64)), jnp.float32)
    factor_c = gaussian(arg_keys[2], (R, K), K ** -0.5, 0.75, ((0, 32), (1, 8)), jnp.float32)
    return {"tensor": tensor, "factor_b": factor_b, "factor_c": factor_c}


EPS = 1e-06
HIGH = lax.Precision.HIGHEST

def gram_of(block):
    return jnp.dot(block.astype(jnp.float32), block.T.astype(jnp.float32), precision=HIGH, preferred_element_type=jnp.float32)

def solve_with(normal, rhs):
    lower = jnp.linalg.cholesky(normal)
    return jax.scipy.linalg.cho_solve((lower, True), rhs)

def unit_rows(raw):
    mean_square = lax.optimization_barrier(jnp.mean(raw * raw, axis=1))
    return raw / jnp.sqrt(mean_square + EPS)[:, None]

def reference(tensor, factor_b, factor_c):
    gram_b = gram_of(factor_b)
    gram_c = gram_of(factor_c)
    normal_a = gram_b * gram_c
    columns_c = factor_c.T

    def step_a(total, item):
        slab, weights = item
        kr_slab = (weights[:, None] * factor_b).astype(jnp.bfloat16)
        return (total + jnp.dot(kr_slab.astype(jnp.float32), slab.T.astype(jnp.float32), preferred_element_type=jnp.float32), None)
    start_a = jnp.zeros((factor_b.shape[0], tensor.shape[1]), jnp.float32)
    mttkrp_a, _ = lax.scan(step_a, start_a, (tensor, columns_c))
    factor_a_new = unit_rows(solve_with(normal_a, mttkrp_a))
    normal_b = gram_of(factor_a_new) * gram_c

    def step_b(total, item):
        slab, weights = item
        kr_slab = (weights[:, None] * factor_a_new).astype(jnp.bfloat16)
        return (total + jnp.dot(kr_slab.astype(jnp.float32), slab.astype(jnp.float32), preferred_element_type=jnp.float32), None)
    start_b = jnp.zeros((factor_b.shape[0], tensor.shape[2]), jnp.float32)
    mttkrp_b, _ = lax.scan(step_b, start_b, (tensor, columns_c))
    factor_b_new = unit_rows(solve_with(normal_b, mttkrp_b))
    return (factor_a_new, factor_b_new)
```

```python
import jax
import jax.numpy as jnp
from jax import lax
from jax.experimental import pallas as pl
from jax.experimental.pallas import tpu as pltpu
from jax.sharding import PartitionSpec as P

EPS = 1e-06
HIGH = lax.Precision.HIGHEST
F32 = jnp.float32
RANK = 32
LANES = 128
NT = (((1,), (1,)), ((), ()))
VMEM = pl.BlockSpec(memory_space=pltpu.VMEM)


def iota(shape, axis):
    return lax.broadcasted_iota(jnp.int32, shape, axis)


def dot_nt(left, right):
    return lax.dot_general(left, right, NT, precision=HIGH, preferred_element_type=F32)


def split(x):
    high = x.astype(jnp.bfloat16)
    return high, (x - high.astype(F32)).astype(jnp.bfloat16)


def inverse(a):
    size = a.shape[0]
    rows, cols = iota(a.shape, 0), iota(a.shape, 1)
    for p in range(size):
        row, col = a[p : p + 1, :], a[:, p : p + 1]
        scale = 1.0 / a[p : p + 1, p : p + 1]
        row = jnp.where(cols[:1] == p, 1.0, row) * scale
        a = jnp.where(cols == p, 0.0, a) - col * row
        a = jnp.where(rows == p, row, a)
    return a


def gather_kernel(y_ref, t_ref, z_ref):
    lane = iota((8, LANES), 1)
    b_rows, c_rows = [], []
    for ia in range(4):
        parts = [y_ref[8 * ia + ka] for ka in range(8)]
        pairs = [
            jnp.where(lane < 64, parts[2 * q], pltpu.roll(parts[2 * q + 1], 64, 1))
            for q in range(4)
        ]
        b_rows.append(jnp.concatenate(pairs, axis=1))
        c_rows.append(sum(parts[1:], parts[0]))
    b = jnp.concatenate(b_rows, axis=0)
    c = jnp.concatenate(c_rows, axis=0)
    gram = dot_nt(b, jnp.concatenate([b, jnp.zeros((96, 512), F32)], axis=0))
    extra = jnp.where(iota((32, LANES), 1) < 64, gram, c)
    high, low = split(b)

    def placed(part, q):
        zeros = jnp.zeros((RANK, 512), jnp.bfloat16)
        return [part if n == q else zeros for n in range(4)]

    weights = jnp.concatenate(
        [jnp.concatenate(placed(high, q) + placed(low, q), axis=0) for q in range(4)], axis=1
    )
    for h in range(2):
        left = jnp.concatenate([t_ref[4 * h + q] for q in range(4)], axis=1)
        both = lax.dot_general(left, weights, NT, preferred_element_type=F32)
        y = both[:, :LANES] + both[:, LANES:]
        for ja in range(8):
            z_ref[ja, 64 * h : 64 * h + 64, :] = y[64 * ja : 64 * ja + 64]
    for ja in range(8):
        z_ref[ja, 128:160, :] = extra


def combine_kernel(z_ref, u_ref, inv_ref, gram_c_ref, c_ref):
    ka = lax.axis_index("ka")
    z = z_ref[0]
    for n in range(1, 8):
        z = z + z_ref[n]
    extra = z[128:160]
    c_all = pltpu.roll(extra, 64, 1)[:, :64]
    gram_c = dot_nt(c_all, c_all)
    gram_c_ref[...] = gram_c
    inv_ref[...] = inverse(extra[:, :32] * gram_c)
    c_here = pltpu.roll(extra, 64 - 8 * ka, 1)
    c_ref[...] = c_here
    c_t = c_here.T[:8]
    c_tiled = jnp.concatenate([c_t] * 4, axis=1)
    which = iota((8, LANES), 0) - iota((8, LANES), 1) // 32
    total = None
    for h in range(2):
        weight = jnp.sum(jnp.where(which == 4 * h, c_tiled, 0.0), axis=0, keepdims=True)
        term = z[64 * h : 64 * h + 64] * weight
        total = term if total is None else total + term
    total = total + pltpu.roll(total, 64, 1)
    total = total + pltpu.roll(total, 32, 1)
    group = iota((16, LANES), 1) // 32
    u = total[:16]
    for q in range(1, 4):
        u = jnp.where(group == q, total[16 * q : 16 * q + 16], u)
    for n in range(8):
        u_ref[n] = u


def solve_kernel(v_ref, inv_ref, x_ref):
    parity = lax.axis_index("ja") % 2
    u = v_ref[0]
    for n in range(1, 8):
        u = u + v_ref[n]
    m_t = jnp.concatenate([u] + [pltpu.roll(u, 128 - 32 * q, 1) for q in range(1, 4)], axis=0)
    m_t = m_t[:, :RANK]
    raw = dot_nt(inv_ref[...], jnp.concatenate([m_t, m_t], axis=0))
    raw = jnp.where(iota((RANK, LANES), 1) // 64 == parity, raw, 0.0)
    for n in range(8):
        x_ref[n] = raw


def second_kernel(x_ref, t_ref, c_ref, w_ref):
    a = jnp.concatenate([x_ref[2 * q] + x_ref[2 * q + 1] for q in range(4)], axis=1)
    zeros = jnp.zeros((RANK, 512), F32)
    extra = dot_nt(a, jnp.concatenate([zeros, zeros, a, zeros], axis=0))
    c = c_ref[...]
    highs, lows = [], []
    for k in range(8):
        high, low = split(a * c[:, k : k + 1])
        highs.append(high)
        lows.append(low)
    left = jnp.concatenate([jnp.concatenate(highs, axis=1), jnp.concatenate(lows, axis=1)], axis=0)
    both = jnp.dot(left, t_ref[...].reshape(4096, 512), preferred_element_type=F32)
    out = both[:RANK] + both[RANK:]
    lane = iota((RANK, LANES), 1)
    for q in range(4):
        pair = out[:, 128 * q : 128 * q + 128]
        even = jnp.where(lane < 64, pair, extra)
        odd = jnp.where(lane < 64, pltpu.roll(pair, 64, 1), extra)
        for ia in range(4):
            w_ref[8 * ia + 2 * q] = even
            w_ref[8 * ia + 2 * q + 1] = odd


def second_solve_kernel(total_i, w_ref, gram_c_ref, raw_ref, scale_ref, ss_ref):
    s = w_ref[0]
    for n in range(1, 32):
        s = s + w_ref[n]
    gram = pltpu.roll(s, 64, 1)[:, :RANK] * 0.125
    diag = jnp.where(iota(gram.shape, 0) == iota(gram.shape, 1), gram, 0.0)
    scale_col = 1.0 / jnp.sqrt(jnp.sum(diag, axis=1, keepdims=True) / total_i + EPS)
    scale_row = 1.0 / jnp.sqrt(jnp.sum(diag, axis=0, keepdims=True) / total_i + EPS)
    inv = inverse(gram * scale_col * scale_row * gram_c_ref[...])
    scale_ref[...] = jnp.broadcast_to(scale_col, (RANK, LANES))
    m = jnp.where(iota(s.shape, 1) < 64, s, 0.0) * scale_col
    raw = jnp.dot(inv, m, precision=HIGH, preferred_element_type=F32)
    raw_ref[...] = raw
    ss = jnp.sum(raw * raw, axis=1, keepdims=True)
    eye = iota((RANK, LANES), 0) == iota((RANK, LANES), 1)
    ss_row = jnp.sum(jnp.where(eye, ss, 0.0), axis=0, keepdims=True)
    ss_ref[...] = jnp.broadcast_to(ss_row[None], ss_ref.shape)


def finish_kernel(total_j, ss_ref, raw_ref, scale_ref, x_ref, out_a_ref, out_b_ref):
    ia, ja, ka = lax.axis_index("ia"), lax.axis_index("ja"), lax.axis_index("ka")
    ss_row = jnp.sum(ss_ref[...], axis=0)
    eye = iota((RANK, LANES), 0) == iota((RANK, LANES), 1)
    ss = jnp.sum(jnp.where(eye, ss_row, 0.0), axis=1, keepdims=True)
    b = raw_ref[...] / jnp.sqrt(ss / total_j + EPS)
    out_b_ref[...] = pltpu.roll(b, 32 - 8 * ia, 0)[:8, :64]
    mine = x_ref[ka]
    mine = (mine + pltpu.roll(mine, 64, 1)) * scale_ref[...]
    out_a_ref[...] = pltpu.roll(mine, 32 - 4 * ja, 0)[:4, :64]


def call(kernel, outs, *args):
    return pl.pallas_call(
        kernel,
        out_shape=[jax.ShapeDtypeStruct(s, F32) for s in outs],
        in_specs=[VMEM] * len(args),
        out_specs=[VMEM] * len(outs),
        compiler_params=pltpu.CompilerParams(vmem_limit_bytes=32 * 1024 * 1024),
    )(*args)


def exchange(x, axes):
    return lax.all_to_all(x, axes, 0, 0, tiled=True)


def body(tensor, factor_b, factor_c):
    total_i = tensor.shape[1] * lax.axis_size("ia")
    total_j = tensor.shape[2] * lax.axis_size("ja")
    ja, ka = lax.axis_index("ja"), lax.axis_index("ka")
    row, lane = iota((8, 64), 0), iota((8, 64), 1)
    c_placed = jnp.where((row == ja) & (lane // 8 == ka), jnp.tile(factor_c, (1, 8)), 0.0)
    start = jnp.concatenate([factor_b, c_placed], axis=1)
    y = exchange(jnp.broadcast_to(start[None], (32, 8, LANES)), ("ia", "ka"))
    (z,) = call(gather_kernel, [(8, 160, LANES)], y, tensor)
    z = exchange(z, "ja")
    u, inv_a, gram_c, c_here = call(
        combine_kernel, [(8, 16, LANES), (RANK, RANK), (RANK, RANK), (RANK, LANES)], z
    )
    v = exchange(u, "ka")
    (x,) = call(solve_kernel, [(8, RANK, LANES)], v, inv_a)
    x = exchange(x, "ja")
    (w,) = call(second_kernel, [(32, RANK, LANES)], x, tensor, c_here)
    w = exchange(w, ("ia", "ka"))
    raw_b, scale_a, ss = call(
        lambda *refs: second_solve_kernel(total_i, *refs),
        [(RANK, LANES), (RANK, LANES), (64, 1, LANES)],
        w,
        gram_c,
    )
    ss = exchange(ss, ("ja", "ka"))
    out_a, out_b = call(
        lambda *refs: finish_kernel(total_j, *refs), [(4, 64), (8, 64)], ss, raw_b, scale_a, x
    )
    return out_a, out_b


def solution(mesh):
    return jax.shard_map(
        body,
        mesh=mesh,
        in_specs=(P("ka", "ia", "ja"), P("ia", ("ja", "ka")), P(("ia", "ja"), "ka")),
        out_specs=(P("ja", ("ia", "ka")), P("ia", ("ja", "ka"))),
        check_vma=False,
    )
```

```python
import jax
import jax.numpy as jnp
from jax import lax
from jax.experimental import pallas as pl
from jax.experimental.pallas import tpu as pltpu
from jax.sharding import PartitionSpec as P

EPS = 1e-06
HIGH = lax.Precision.HIGHEST
F32 = jnp.float32
RANK = 32
LANES = 128
NT = (((1,), (1,)), ((), ()))
VMEM = pl.BlockSpec(memory_space=pltpu.VMEM)
HBM = pl.BlockSpec(memory_space=pltpu.HBM)
KEPT = 6


def iota(shape, axis):
    return lax.broadcasted_iota(jnp.int32, shape, axis)


def dot_nt(left, right):
    return lax.dot_general(left, right, NT, precision=HIGH, preferred_element_type=F32)


def split(x):
    high = x.astype(jnp.bfloat16)
    return high, (x - high.astype(F32)).astype(jnp.bfloat16)


def fold(x):
    n = x.shape[0] // 4
    group = iota((n, LANES), 1) // 32
    out = x[:n]
    for q in range(1, 4):
        out = jnp.where(group == q, x[n * q : n * q + n], out)
    return out


def unfold(x):
    parts = [x] + [pltpu.roll(x, LANES - 32 * q, 1) for q in range(1, 4)]
    return jnp.concatenate(parts, axis=0)[:, :32]


def total(ref, *index):
    out = ref[(0, *index)]
    for n in range(1, ref.shape[0]):
        out = out + ref[(n, *index)]
    return out


def folded_gram(x):
    return fold(dot_nt(x, jnp.concatenate([x] * 4, axis=0)))


def inverse(a):
    size = a.shape[0]
    rows, cols = iota(a.shape, 0), iota(a.shape, 1)
    for p in range(size):
        row, col = a[p : p + 1, :], a[:, p : p + 1]
        scale = 1.0 / a[p : p + 1, p : p + 1]
        row = jnp.where(cols[:1] == p, 1.0, row) * scale
        a = jnp.where(cols == p, 0.0, a) - col * row
        a = jnp.where(rows == p, row, a)
    return a


def fetch(t_ref, places, sems):
    copies = [
        pltpu.make_async_copy(t_ref.at[KEPT + n], places.at[n], sems.at[n])
        for n in range(t_ref.shape[0] - KEPT)
    ]
    for copy in copies:
        copy.start()
    return copies


def load_kernel(t_ref, *refs):
    sems = refs[-1]
    copies = [pltpu.make_async_copy(t_ref.at[k], refs[k], sems.at[k]) for k in range(KEPT)]
    for copy in copies:
        copy.start()
    for copy in copies:
        copy.wait()


def start_kernel(b_hbm, c_hbm, y_ref, b_ref, c_ref, sems):
    copies = [
        pltpu.make_async_copy(b_hbm, b_ref, sems.at[0]),
        pltpu.make_async_copy(c_hbm, c_ref, sems.at[1]),
    ]
    for copy in copies:
        copy.start()
    for copy in copies:
        copy.wait()
    ja, ka = lax.axis_index("ja"), lax.axis_index("ka")
    row, lane = iota((8, LANES), 0), iota((8, LANES), 1)
    c_tiled = jnp.concatenate([c_ref[...]] * 16, axis=1)
    c_placed = jnp.where((row == ja) & (lane // 8 == 8 + ka), c_tiled, 0.0)
    b_wide = jnp.concatenate([b_ref[...], jnp.zeros((8, 64), F32)], axis=1)
    tile = jnp.where(lane < 64, b_wide, c_placed)
    for n in range(32):
        y_ref[n] = tile


def first_kernel(t_hbm, y_ref, *refs):
    keep_ref, send_ref, scratch, rest, sems = refs[KEPT:]
    copies = fetch(t_hbm, rest, sems)
    steps = [*refs[:KEPT], *(rest.at[n] for n in range(8 - KEPT))]
    core = lax.axis_index("ja") % 2
    lane = iota((8, LANES), 1)
    b_rows, c_rows = [], []
    for ia in range(4):
        parts = [y_ref[8 * ia + ka] for ka in range(8)]
        pairs = [
            jnp.where(lane < 64, parts[2 * q], pltpu.roll(parts[2 * q + 1], 64, 1))
            for q in range(4)
        ]
        b_rows.append(jnp.concatenate(pairs, axis=1))
        c_rows.append(sum(parts[1:], parts[0]))
    b = jnp.concatenate(b_rows, axis=0)
    c = jnp.concatenate(c_rows, axis=0)
    gram = dot_nt(b, jnp.concatenate([b, jnp.zeros((96, 512), F32)], axis=0))
    extra = jnp.where(iota((32, LANES), 1) < 64, gram, c)
    high, low = split(b)

    def placed(part, q):
        zeros = jnp.zeros((RANK, 512), jnp.bfloat16)
        return [part if n == q else zeros for n in range(4)]

    weights = jnp.concatenate(
        [jnp.concatenate(placed(high, q) + placed(low, q), axis=0) for q in range(4)], axis=1
    )
    for h in range(2):
        if h == 1:
            for copy in copies:
                copy.wait()
        left = jnp.concatenate([steps[4 * h + q][...] for q in range(4)], axis=1)
        both = lax.dot_general(left, weights, NT, preferred_element_type=F32)
        scratch[h] = both[:, :LANES] + both[:, LANES:]
    for n in range(4):
        for ref, which in ((keep_ref, core), (send_ref, 1 - core)):
            start = pl.multiple_of(64 * (2 * n + which), 64)
            for h in range(2):
                ref[n, 64 * h : 64 * h + 64, :] = scratch[h, pl.ds(start, 64), :]
            ref[n, 128:160, :] = extra


def combine_kernel(z_ref, u_ref, gram_ref, c_all_ref, c_ref):
    ka = lax.axis_index("ka")
    z = total(z_ref)
    extra = z[128:160]
    gram_ref[...] = extra[:, :32]
    c_all_ref[...] = pltpu.roll(extra, 64, 1)[:, :64]
    c_here = pltpu.roll(extra, 64 - 8 * ka, 1)
    c_ref[...] = c_here
    c_t = c_here.T[:8]
    c_tiled = jnp.concatenate([c_t] * 4, axis=1)
    which = iota((8, LANES), 0) - iota((8, LANES), 1) // 32
    acc = None
    for h in range(2):
        weight = jnp.sum(jnp.where(which == 4 * h, c_tiled, 0.0), axis=0, keepdims=True)
        term = z[64 * h : 64 * h + 64] * weight
        acc = term if acc is None else acc + term
    acc = acc + pltpu.roll(acc, 64, 1)
    acc = acc + pltpu.roll(acc, 32, 1)
    u = fold(acc)
    for n in range(8):
        u_ref[n] = u


def invert_a_kernel(gram_b_ref, c_all_ref, inv_ref, gram_c_ref):
    gram_c = dot_nt(c_all_ref[...], c_all_ref[...])
    gram_c_ref[...] = gram_c
    inv_ref[...] = inverse(gram_b_ref[...] * gram_c)


def solve_kernel(v_ref, inv_ref, x_ref):
    parity = lax.axis_index("ja") % 2
    m_t = unfold(total(v_ref))
    raw = dot_nt(inv_ref[...], jnp.concatenate([m_t, m_t], axis=0))
    raw = jnp.where(iota((RANK, LANES), 1) // 64 == parity, raw, 0.0)
    for n in range(8):
        x_ref[n] = raw


def second_kernel(t_hbm, x_ref, c_ref, *refs):
    w_ref, g_ref, rest, sems = refs[KEPT:]
    copies = fetch(t_hbm, rest, sems)
    steps = [*refs[:KEPT], *(rest.at[n] for n in range(8 - KEPT))]
    a = jnp.concatenate([x_ref[2 * q] + x_ref[2 * q + 1] for q in range(4)], axis=1)
    g_ref[...] = folded_gram(a)
    c = c_ref[...]
    highs, lows = [], []
    for k in range(8):
        high, low = split(a * c[:, k : k + 1])
        highs.append(high)
        lows.append(low)
    left = jnp.concatenate([jnp.concatenate(highs, axis=1), jnp.concatenate(lows, axis=1)], axis=0)
    for copy in copies:
        copy.wait()
    right = jnp.concatenate([ref[...] for ref in steps], axis=0)
    both = jnp.dot(left, right, preferred_element_type=F32)
    out = both[:RANK] + both[RANK:]
    low_lanes = iota((16, LANES), 1) < 64
    for q in range(4):
        pair = out[:, 128 * q : 128 * q + 128]
        turned = pltpu.roll(pair, 64, 1)
        even = jnp.where(low_lanes, pair[:16], turned[16:])
        odd = jnp.where(low_lanes, turned[:16], pair[16:])
        for ia in range(4):
            w_ref[8 * ia + 2 * q] = even
            w_ref[8 * ia + 2 * q + 1] = odd


def invert_b_kernel(total_i, g0_ref, g1_ref, g2_ref, g3_ref, gram_c_ref, inv_ref, scale_ref):
    gram = unfold((g0_ref[...] + g1_ref[...]) + (g2_ref[...] + g3_ref[...]))
    diag = jnp.where(iota(gram.shape, 0) == iota(gram.shape, 1), gram, 0.0)
    scale_col = 1.0 / jnp.sqrt(jnp.sum(diag, axis=1, keepdims=True) / total_i + EPS)
    scale_row = 1.0 / jnp.sqrt(jnp.sum(diag, axis=0, keepdims=True) / total_i + EPS)
    inv_ref[...] = inverse(gram * scale_col * scale_row * gram_c_ref[...])
    scale_ref[...] = jnp.broadcast_to(scale_col, (RANK, LANES))


def second_solve_kernel(w_ref, inv_ref, scale_ref, raw_ref, ss_ref):
    s = total(w_ref)
    m = jnp.concatenate([s, pltpu.roll(s, 64, 1)], axis=0) * scale_ref[...]
    raw = jnp.dot(inv_ref[...], m, precision=HIGH, preferred_element_type=F32)
    raw_ref[...] = raw
    square = jnp.where(iota(raw.shape, 1) < 64, raw * raw, 0.0)
    ss = jnp.sum(square, axis=1, keepdims=True)
    eye = iota((RANK, LANES), 0) == iota((RANK, LANES), 1)
    ss_row = jnp.sum(jnp.where(eye, ss, 0.0), axis=0, keepdims=True)
    ss_ref[...] = jnp.broadcast_to(ss_row, ss_ref.shape)


def finish_kernel(total_j, ss_ref, raw_ref, scale_ref, x_ref, out_a_ref, out_b_ref):
    ia, ja, ka = lax.axis_index("ia"), lax.axis_index("ja"), lax.axis_index("ka")
    ss_row = jnp.sum(ss_ref[...], axis=0, keepdims=True)
    eye = iota((RANK, LANES), 0) == iota((RANK, LANES), 1)
    ss = jnp.sum(jnp.where(eye, ss_row, 0.0), axis=1, keepdims=True)
    b = raw_ref[...] / jnp.sqrt(ss / total_j + EPS)
    out_b_ref[...] = pltpu.roll(b, 32 - 8 * ia, 0)[:8, :64]
    mine = x_ref[ka]
    mine = (mine + pltpu.roll(mine, 64, 1)) * scale_ref[...]
    out_a_ref[...] = pltpu.roll(mine, 32 - 4 * ja, 0)[:4, :64]


def call(kernel, outs, *args, scratch=()):
    big = [a.ndim == 3 and a.dtype == jnp.bfloat16 for a in args]
    return pl.pallas_call(
        kernel,
        out_shape=[jax.ShapeDtypeStruct(s, F32) for s in outs],
        in_specs=[HBM if flag else VMEM for flag in big],
        out_specs=[VMEM] * len(outs),
        scratch_shapes=scratch,
        compiler_params=pltpu.CompilerParams(vmem_limit_bytes=32 * 1024 * 1024),
    )(*args)


def load(tensor):
    step = tensor.shape[1:]
    return pl.pallas_call(
        load_kernel,
        out_shape=[pltpu.VMEM(step, tensor.dtype)] * KEPT,
        in_specs=[HBM],
        out_specs=[VMEM] * KEPT,
        scratch_shapes=[pltpu.SemaphoreType.DMA((KEPT,))],
        compiler_params=pltpu.CompilerParams(vmem_limit_bytes=32 * 1024 * 1024),
    )(tensor)


def rest_scratch(tensor):
    count = tensor.shape[0] - KEPT
    return [
        pltpu.VMEM((count, *tensor.shape[1:]), tensor.dtype),
        pltpu.SemaphoreType.DMA((count,)),
    ]


def exchange(x, axes, groups=None):
    return lax.all_to_all(x, axes, 0, 0, tiled=True, axis_index_groups=groups)


def turned(x, axis, step):
    size = lax.axis_size(axis)
    return lax.ppermute(x, axis, [(n, (n + step) % size) for n in range(size)])


def body(tensor, factor_b, factor_c):
    total_i = tensor.shape[1] * lax.axis_size("ia")
    total_j = tensor.shape[2] * lax.axis_size("ja")
    tensor, factor_b, factor_c = (
        pltpu.with_memory_space_constraint(a, pltpu.HBM) for a in (tensor, factor_b, factor_c)
    )
    (y,) = pl.pallas_call(
        start_kernel,
        out_shape=[jax.ShapeDtypeStruct((32, 8, LANES), F32)],
        in_specs=[HBM, HBM],
        out_specs=[VMEM],
        scratch_shapes=[
            pltpu.VMEM(factor_b.shape, F32),
            pltpu.VMEM(factor_c.shape, F32),
            pltpu.SemaphoreType.DMA((2,)),
        ],
    )(factor_b, factor_c)
    y = exchange(y, ("ia", "ka"))
    steps = load(tensor)
    keep, send = call(
        first_kernel,
        [(4, 160, LANES), (4, 160, LANES)],
        tensor,
        y,
        *steps,
        scratch=[pltpu.VMEM((2, 512, LANES), F32), *rest_scratch(tensor)],
    )
    z = keep + lax.ppermute(send, "ja", [(n, n ^ 1) for n in range(8)])
    z = exchange(z, "ja", [[0, 2, 4, 6], [1, 3, 5, 7]])
    u, gram_b, c_all, c_here = call(
        combine_kernel, [(8, 16, LANES), (RANK, RANK), (RANK, 64), (RANK, LANES)], z
    )
    v = exchange(u, "ka")
    inv_a, gram_c = call(invert_a_kernel, [(RANK, RANK), (RANK, RANK)], gram_b, c_all)
    (x,) = call(solve_kernel, [(8, RANK, LANES)], v, inv_a)
    x = exchange(x, "ja")
    w, g = call(
        second_kernel,
        [(32, 16, LANES), (8, LANES)],
        tensor,
        x,
        c_here,
        *steps,
        scratch=rest_scratch(tensor),
    )
    w = exchange(w, ("ia", "ka"))
    inv_b, scale_a = call(
        lambda *refs: invert_b_kernel(total_i, *refs),
        [(RANK, RANK), (RANK, LANES)],
        g,
        *(turned(g, "ia", step) for step in (1, 2, 3)),
        gram_c,
    )
    raw_b, ss = call(second_solve_kernel, [(RANK, LANES), (64, LANES)], w, inv_b, scale_a)
    ss = exchange(ss.reshape(64, 1, LANES), ("ja", "ka")).reshape(64, LANES)
    out_a, out_b = call(
        lambda *refs: finish_kernel(total_j, *refs), [(4, 64), (8, 64)], ss, raw_b, scale_a, x
    )
    return out_a, out_b


def solution(mesh):
    return jax.shard_map(
        body,
        mesh=mesh,
        in_specs=(P("ka", "ia", "ja"), P("ia", ("ja", "ka")), P(("ia", "ja"), "ka")),
        out_specs=(P("ja", ("ia", "ka")), P("ia", ("ja", "ka"))),
        check_vma=False,
    )
```

```python
import jax
import jax.numpy as jnp
from jax import lax
from jax.experimental import pallas as pl
from jax.experimental.pallas import tpu as pltpu
from jax.sharding import PartitionSpec as P

EPS = 1e-06
HIGH = lax.Precision.HIGHEST
F32 = jnp.float32
RANK = 32
LANES = 128
NT = (((1,), (1,)), ((), ()))
VMEM = pl.BlockSpec(memory_space=pltpu.VMEM)
HBM = pl.BlockSpec(memory_space=pltpu.HBM)
LONG = pl.CostEstimate(flops=10**10, bytes_accessed=0, transcendentals=0)


def iota(shape, axis):
    return lax.broadcasted_iota(jnp.int32, shape, axis)


def dot_nt(left, right):
    return lax.dot_general(left, right, NT, precision=HIGH, preferred_element_type=F32)


def split(x):
    high = x.astype(jnp.bfloat16)
    return high, (x - high.astype(F32)).astype(jnp.bfloat16)


def fold(x):
    n = x.shape[0] // 4
    group = iota((n, LANES), 1) // 32
    out = x[:n]
    for q in range(1, 4):
        out = jnp.where(group == q, x[n * q : n * q + n], out)
    return out


def unfold(x):
    parts = [x] + [pltpu.roll(x, LANES - 32 * q, 1) for q in range(1, 4)]
    return jnp.concatenate(parts, axis=0)[:, :32]


def total(ref, *index):
    out = ref[(0, *index)]
    for n in range(1, ref.shape[0]):
        out = out + ref[(n, *index)]
    return out


def folded_gram(x):
    return fold(dot_nt(x, jnp.concatenate([x] * 4, axis=0)))


def inverse(a):
    size = a.shape[0]
    rows, cols = iota(a.shape, 0), iota(a.shape, 1)
    for start in range(0, size, size // 2):
        spread = {p: jnp.broadcast_to(a[:, p : p + 1], a.shape) for p in range(start, start + size // 2)}
        for p in range(start, start + size // 2):
            col = spread.pop(p)
            scale = 1.0 / col[p : p + 1, :]
            row = jnp.where(cols[:1] == p, 1.0, a[p : p + 1, :]) * scale
            a = jnp.where(cols == p, 0.0, a) - col * row
            a = jnp.where(rows == p, row, a)
            for q, other in spread.items():
                there = other[p : p + 1, :] * scale
                spread[q] = jnp.where(rows == p, there, other - col * there)
    return a


def start_kernel(b_hbm, c_hbm, y_ref, b_ref, c_ref, sems):
    copies = [
        pltpu.make_async_copy(b_hbm, b_ref, sems.at[0]),
        pltpu.make_async_copy(c_hbm, c_ref, sems.at[1]),
    ]
    for copy in copies:
        copy.start()
    for copy in copies:
        copy.wait()
    ja, ka = lax.axis_index("ja"), lax.axis_index("ka")
    row, lane = iota((8, LANES), 0), iota((8, LANES), 1)
    c_tiled = jnp.concatenate([c_ref[...]] * 16, axis=1)
    c_placed = jnp.where((row == ja) & (lane // 8 == 8 + ka), c_tiled, 0.0)
    b_wide = jnp.concatenate([b_ref[...], jnp.zeros((8, 64), F32)], axis=1)
    tile = jnp.where(lane < 64, b_wide, c_placed)
    for n in range(32):
        y_ref[n] = tile


def first_kernel(y_ref, t_ref, keep_ref, send_ref, scratch):
    core = lax.axis_index("ja") % 2
    lane = iota((8, LANES), 1)
    b_rows, c_rows = [], []
    for ia in range(4):
        parts = [y_ref[8 * ia + ka] for ka in range(8)]
        pairs = [
            jnp.where(lane < 64, parts[2 * q], pltpu.roll(parts[2 * q + 1], 64, 1))
            for q in range(4)
        ]
        b_rows.append(jnp.concatenate(pairs, axis=1))
        c_rows.append(sum(parts[1:], parts[0]))
    b = jnp.concatenate(b_rows, axis=0)
    c = jnp.concatenate(c_rows, axis=0)
    gram = dot_nt(b, jnp.concatenate([b, jnp.zeros((96, 512), F32)], axis=0))
    extra = jnp.where(iota((32, LANES), 1) < 64, gram, c)
    high, low = split(b)

    def placed(part, q):
        zeros = jnp.zeros((RANK, 512), jnp.bfloat16)
        return [part if n == q else zeros for n in range(4)]

    weights = jnp.concatenate(
        [jnp.concatenate(placed(high, q) + placed(low, q), axis=0) for q in range(4)], axis=1
    )
    for h in range(2):
        left = jnp.concatenate([t_ref[4 * h + q] for q in range(4)], axis=1)
        both = lax.dot_general(left, weights, NT, preferred_element_type=F32)
        scratch[h] = both[:, :LANES] + both[:, LANES:]
    for n in range(4):
        for ref, which in ((keep_ref, core), (send_ref, 1 - core)):
            start = pl.multiple_of(64 * (2 * n + which), 64)
            for h in range(2):
                ref[n, 64 * h : 64 * h + 64, :] = scratch[h, pl.ds(start, 64), :]
            ref[n, 128:160, :] = extra


def combine_kernel(z_ref, u_ref, gram_ref, c_all_ref, c_ref):
    ka = lax.axis_index("ka")
    z = total(z_ref)
    extra = z[128:160]
    gram_ref[...] = extra[:, :32]
    c_all_ref[...] = pltpu.roll(extra, 64, 1)[:, :64]
    c_here = pltpu.roll(extra, 64 - 8 * ka, 1)
    c_ref[...] = c_here
    c_t = c_here.T[:8]
    c_tiled = jnp.concatenate([c_t] * 4, axis=1)
    which = iota((8, LANES), 0) - iota((8, LANES), 1) // 32
    acc = None
    for h in range(2):
        weight = jnp.sum(jnp.where(which == 4 * h, c_tiled, 0.0), axis=0, keepdims=True)
        term = z[64 * h : 64 * h + 64] * weight
        acc = term if acc is None else acc + term
    acc = acc + pltpu.roll(acc, 64, 1)
    acc = acc + pltpu.roll(acc, 32, 1)
    u = fold(acc)
    for n in range(8):
        u_ref[n] = u


def invert_a_kernel(gram_b_ref, c_all_ref, inv_ref, gram_c_ref):
    gram_c = dot_nt(c_all_ref[...], c_all_ref[...])
    gram_c_ref[...] = gram_c
    inv_ref[...] = inverse(gram_b_ref[...] * gram_c)


def solve_kernel(v_ref, inv_ref, x_ref):
    m_t = unfold(total(v_ref))
    raw = dot_nt(inv_ref[...], jnp.concatenate([m_t, m_t], axis=0))
    raw = jnp.where(iota((16, LANES), 1) < 64, raw[:16], raw[16:])
    for n in range(8):
        x_ref[n] = raw


def second_kernel(x_ref, t_ref, c_ref, w_ref, g_ref):
    low_lanes = iota((16, LANES), 1) < 64
    parts = []
    for q in range(4):
        one, two = x_ref[2 * q], x_ref[2 * q + 1]
        top = jnp.where(low_lanes, one, pltpu.roll(two, 64, 1))
        bottom = jnp.where(low_lanes, pltpu.roll(one, 64, 1), two)
        parts.append(jnp.concatenate([top, bottom], axis=0))
    a = jnp.concatenate(parts, axis=1)
    g_ref[...] = folded_gram(a)
    c = c_ref[...]
    highs, lows = [], []
    for k in range(8):
        high, low = split(a * c[:, k : k + 1])
        highs.append(high)
        lows.append(low)
    left = jnp.concatenate([jnp.concatenate(highs, axis=1), jnp.concatenate(lows, axis=1)], axis=0)
    both = jnp.dot(left, t_ref[...].reshape(4096, 512), preferred_element_type=F32)
    out = both[:RANK] + both[RANK:]
    for q in range(4):
        pair = out[:, 128 * q : 128 * q + 128]
        turned = pltpu.roll(pair, 64, 1)
        even = jnp.where(low_lanes, pair[:16], turned[16:])
        odd = jnp.where(low_lanes, turned[:16], pair[16:])
        for ia in range(4):
            w_ref[8 * ia + 2 * q] = even
            w_ref[8 * ia + 2 * q + 1] = odd


def invert_b_kernel(total_i, g0_ref, g1_ref, g2_ref, g3_ref, gram_c_ref, inv_ref, scale_ref):
    gram = unfold((g0_ref[...] + g1_ref[...]) + (g2_ref[...] + g3_ref[...]))
    diag = jnp.where(iota(gram.shape, 0) == iota(gram.shape, 1), gram, 0.0)
    scale_col = 1.0 / jnp.sqrt(jnp.sum(diag, axis=1, keepdims=True) / total_i + EPS)
    scale_row = 1.0 / jnp.sqrt(jnp.sum(diag, axis=0, keepdims=True) / total_i + EPS)
    inv_ref[...] = inverse(gram * scale_col * scale_row * gram_c_ref[...])
    scale_ref[...] = jnp.broadcast_to(scale_col, (RANK, LANES))


def second_solve_kernel(w_ref, inv_ref, scale_ref, raw_ref, ss_ref):
    s = total(w_ref)
    m = jnp.concatenate([s, pltpu.roll(s, 64, 1)], axis=0) * scale_ref[...]
    raw = jnp.dot(inv_ref[...], m, precision=HIGH, preferred_element_type=F32)
    raw_ref[...] = raw
    square = jnp.where(iota(raw.shape, 1) < 64, raw * raw, 0.0)
    ss = jnp.sum(square, axis=1, keepdims=True)
    eye = iota((RANK, LANES), 0) == iota((RANK, LANES), 1)
    ss_row = jnp.sum(jnp.where(eye, ss, 0.0), axis=0, keepdims=True)
    ss_ref[...] = jnp.broadcast_to(ss_row, ss_ref.shape)


def finish_kernel(total_j, ss_ref, raw_ref, scale_ref, x_ref, out_a_ref, out_b_ref):
    ia, ja, ka = lax.axis_index("ia"), lax.axis_index("ja"), lax.axis_index("ka")
    ss_row = jnp.sum(ss_ref[...], axis=0, keepdims=True)
    eye = iota((RANK, LANES), 0) == iota((RANK, LANES), 1)
    ss = jnp.sum(jnp.where(eye, ss_row, 0.0), axis=1, keepdims=True)
    b = raw_ref[...] / jnp.sqrt(ss / total_j + EPS)
    out_b_ref[...] = pltpu.roll(b, 32 - 8 * ia, 0)[:8, :64]
    mine = x_ref[ka]
    mine = jnp.concatenate([mine, pltpu.roll(mine, 64, 1)], axis=0) * scale_ref[...]
    out_a_ref[...] = pltpu.roll(mine, 32 - 4 * ja, 0)[:4, :64]


def call(kernel, outs, *args, scratch=(), cost=None, space=VMEM):
    return pl.pallas_call(
        kernel,
        out_shape=[jax.ShapeDtypeStruct(s, F32) for s in outs],
        in_specs=[space] * len(args),
        out_specs=[VMEM] * len(outs),
        scratch_shapes=scratch,
        cost_estimate=cost,
        compiler_params=pltpu.CompilerParams(vmem_limit_bytes=32 * 1024 * 1024),
    )(*args)


def exchange(x, axes, groups=None):
    return lax.all_to_all(x, axes, 0, 0, tiled=True, axis_index_groups=groups)


def turned(x, axis, step):
    size = lax.axis_size(axis)
    return lax.ppermute(x, axis, [(n, (n + step) % size) for n in range(size)])


def body(tensor, factor_b, factor_c):
    total_i = tensor.shape[1] * lax.axis_size("ia")
    total_j = tensor.shape[2] * lax.axis_size("ja")
    factor_b, factor_c = (
        pltpu.with_memory_space_constraint(a, pltpu.HBM) for a in (factor_b, factor_c)
    )
    (y,) = call(
        start_kernel,
        [(32, 8, LANES)],
        factor_b,
        factor_c,
        scratch=[
            pltpu.VMEM(factor_b.shape, F32),
            pltpu.VMEM(factor_c.shape, F32),
            pltpu.SemaphoreType.DMA((2,)),
        ],
        cost=LONG,
        space=HBM,
    )
    y = exchange(y, ("ia", "ka"))
    keep, send = call(
        first_kernel,
        [(4, 160, LANES), (4, 160, LANES)],
        y,
        tensor,
        scratch=[pltpu.VMEM((2, 512, LANES), F32)],
    )
    z = keep + lax.ppermute(send, "ja", [(n, n ^ 1) for n in range(8)])
    z = exchange(z, "ja", [[0, 2, 4, 6], [1, 3, 5, 7]])
    u, gram_b, c_all, c_here = call(
        combine_kernel, [(8, 16, LANES), (RANK, RANK), (RANK, 64), (RANK, LANES)], z
    )
    v = exchange(u, "ka")
    inv_a, gram_c = call(invert_a_kernel, [(RANK, RANK), (RANK, RANK)], gram_b, c_all)
    (x,) = call(solve_kernel, [(8, 16, LANES)], v, inv_a, cost=LONG)
    x = exchange(x, "ja")
    w, g = call(second_kernel, [(32, 16, LANES), (8, LANES)], x, tensor, c_here)
    w = exchange(w, ("ia", "ka"))
    inv_b, scale_a = call(
        lambda *refs: invert_b_kernel(total_i, *refs),
        [(RANK, RANK), (RANK, LANES)],
        g,
        *(turned(g, "ia", step) for step in (1, 2, 3)),
        gram_c,
    )
    raw_b, ss = call(second_solve_kernel, [(RANK, LANES), (64, LANES)], w, inv_b, scale_a)
    ss = exchange(ss.reshape(64, 1, LANES), ("ja", "ka")).reshape(64, LANES)
    out_a, out_b = call(
        lambda *refs: finish_kernel(total_j, *refs), [(4, 64), (8, 64)], ss, raw_b, scale_a, x
    )
    return out_a, out_b


def solution(mesh):
    return jax.shard_map(
        body,
        mesh=mesh,
        in_specs=(P("ka", "ia", "ja"), P("ia", ("ja", "ka")), P(("ia", "ja"), "ka")),
        out_specs=(P("ja", ("ia", "ka")), P("ia", ("ja", "ka"))),
        check_vma=False,
    )
```

```python
import jax
import jax.numpy as jnp
from jax import lax
from jax.experimental import pallas as pl
from jax.experimental.pallas import tpu as pltpu
from jax.sharding import PartitionSpec as P

EPS = 1e-06
HIGH = lax.Precision.HIGHEST
F32 = jnp.float32
RANK = 32
LANES = 128
NT = (((1,), (1,)), ((), ()))
VMEM = pl.BlockSpec(memory_space=pltpu.VMEM)
HBM = pl.BlockSpec(memory_space=pltpu.HBM)
LONG = pl.CostEstimate(flops=10**10, bytes_accessed=0, transcendentals=0)


def iota(shape, axis):
    return lax.broadcasted_iota(jnp.int32, shape, axis)


def dot_nt(left, right):
    return lax.dot_general(left, right, NT, precision=HIGH, preferred_element_type=F32)


def split(x):
    high = x.astype(jnp.bfloat16)
    return high, (x - high.astype(F32)).astype(jnp.bfloat16)


def fold(x):
    n = x.shape[0] // 4
    group = iota((n, LANES), 1) // 32
    out = x[:n]
    for q in range(1, 4):
        out = jnp.where(group == q, x[n * q : n * q + n], out)
    return out


def unfold(x):
    parts = [x] + [pltpu.roll(x, LANES - 32 * q, 1) for q in range(1, 4)]
    return jnp.concatenate(parts, axis=0)[:, :32]


def total(ref, *index):
    out = ref[(0, *index)]
    for n in range(1, ref.shape[0]):
        out = out + ref[(n, *index)]
    return out


def folded_gram(x):
    return fold(dot_nt(x, jnp.concatenate([x] * 4, axis=0)))


def inverse(a):
    size = a.shape[0]
    rows, cols = iota(a.shape, 0), iota(a.shape, 1)
    for start in range(0, size, size // 2):
        spread = {p: jnp.broadcast_to(a[:, p : p + 1], a.shape) for p in range(start, start + size // 2)}
        for p in range(start, start + size // 2):
            col = spread.pop(p)
            scale = 1.0 / col[p : p + 1, :]
            row = jnp.where(cols[:1] == p, 1.0, a[p : p + 1, :]) * scale
            a = jnp.where(cols == p, 0.0, a) - col * row
            a = jnp.where(rows == p, row, a)
            for q, other in spread.items():
                there = other[p : p + 1, :] * scale
                spread[q] = jnp.where(rows == p, there, other - col * there)
    return a


def start_kernel(b_hbm, c_hbm, y_ref, b_ref, c_ref, sems):
    copies = [
        pltpu.make_async_copy(b_hbm, b_ref, sems.at[0]),
        pltpu.make_async_copy(c_hbm, c_ref, sems.at[1]),
    ]
    for copy in copies:
        copy.start()
    for copy in copies:
        copy.wait()
    ja, ka = lax.axis_index("ja"), lax.axis_index("ka")
    row, lane = iota((8, LANES), 0), iota((8, LANES), 1)
    c_tiled = jnp.concatenate([c_ref[...]] * 16, axis=1)
    c_placed = jnp.where((row == ja) & (lane // 8 == 8 + ka), c_tiled, 0.0)
    b_wide = jnp.concatenate([b_ref[...], jnp.zeros((8, 64), F32)], axis=1)
    tile = jnp.where(lane < 64, b_wide, c_placed)
    for n in range(32):
        y_ref[n] = tile


def first_kernel(y_ref, t_ref, keep_ref, send_ref, scratch):
    core = lax.axis_index("ja") % 2
    lane = iota((8, LANES), 1)
    b_rows, c_rows = [], []
    for ia in range(4):
        parts = [y_ref[8 * ia + ka] for ka in range(8)]
        pairs = [
            jnp.where(lane < 64, parts[2 * q], pltpu.roll(parts[2 * q + 1], 64, 1))
            for q in range(4)
        ]
        b_rows.append(jnp.concatenate(pairs, axis=1))
        c_rows.append(sum(parts[1:], parts[0]))
    b = jnp.concatenate(b_rows, axis=0)
    c = jnp.concatenate(c_rows, axis=0)
    gram = dot_nt(b, jnp.concatenate([b, jnp.zeros((96, 512), F32)], axis=0))
    extra = jnp.where(iota((32, LANES), 1) < 64, gram, c)
    high, low = split(b)

    def placed(part, q):
        zeros = jnp.zeros((RANK, 512), jnp.bfloat16)
        return [part if n == q else zeros for n in range(4)]

    weights = jnp.concatenate(
        [jnp.concatenate(placed(high, q) + placed(low, q), axis=0) for q in range(4)], axis=1
    )
    for h in range(2):
        left = jnp.concatenate([t_ref[4 * h + q] for q in range(4)], axis=1)
        both = lax.dot_general(left, weights, NT, preferred_element_type=F32)
        scratch[h] = both[:, :LANES] + both[:, LANES:]
    for n in range(4):
        for ref, which in ((keep_ref, core), (send_ref, 1 - core)):
            start = pl.multiple_of(64 * (2 * n + which), 64)
            for h in range(2):
                ref[n, 64 * h : 64 * h + 64, :] = scratch[h, pl.ds(start, 64), :]
            ref[n, 128:160, :] = extra


def combine_kernel(z_ref, u_ref, gram_ref, c_all_ref, c_ref):
    ka = lax.axis_index("ka")
    z = total(z_ref)
    extra = z[128:160]
    gram_ref[...] = extra[:, :32]
    c_all_ref[...] = pltpu.roll(extra, 64, 1)[:, :64]
    c_here = pltpu.roll(extra, 64 - 8 * ka, 1)
    c_ref[...] = c_here
    c_t = c_here.T[:8]
    c_tiled = jnp.concatenate([c_t] * 4, axis=1)
    which = iota((8, LANES), 0) - iota((8, LANES), 1) // 32
    acc = None
    for h in range(2):
        weight = jnp.sum(jnp.where(which == 4 * h, c_tiled, 0.0), axis=0, keepdims=True)
        term = z[64 * h : 64 * h + 64] * weight
        acc = term if acc is None else acc + term
    acc = acc + pltpu.roll(acc, 64, 1)
    acc = acc + pltpu.roll(acc, 32, 1)
    u = fold(acc)
    for n in range(32):
        u_ref[n] = u


def invert_a_kernel(gram_b_ref, c_all_ref, inv_ref, gram_c_ref):
    gram_c = dot_nt(c_all_ref[...], c_all_ref[...])
    gram_c_ref[...] = gram_c
    inv_ref[...] = inverse(gram_b_ref[...] * gram_c)


def turn_kernel(v_ref, m_ref):
    parts = []
    for y in range(4):
        part = v_ref[8 * y]
        for ka in range(1, 8):
            part = part + v_ref[8 * y + ka]
        parts.append(unfold(part))
    m_ref[...] = jnp.concatenate(parts, axis=0).T


def second_kernel(mine_ref, other_ref, inv_ref, t_ref, c_ref, w_ref, g_ref, a_ref, scratch):
    ka, core = lax.axis_index("ka"), lax.axis_index("ja") % 2
    low_lanes = iota((RANK, LANES), 1) < 64
    even = jnp.where(core == 0, mine_ref[...], other_ref[...])
    odd = jnp.where(core == 0, other_ref[...], mine_ref[...])
    parts = []
    for p in range(2):
        one, two = even[:, 128 * p : 128 * p + 128], odd[:, 128 * p : 128 * p + 128]
        parts.append(jnp.where(low_lanes, one, pltpu.roll(two, 64, 1)))
        parts.append(jnp.where(low_lanes, pltpu.roll(one, 64, 1), two))
    m = jnp.concatenate(parts, axis=1)
    a = jnp.dot(inv_ref[...], m, precision=HIGH, preferred_element_type=F32)
    for q in range(4):
        pair = a[:, 128 * q : 128 * q + 128]
        scratch[2 * q] = pair
        scratch[2 * q + 1] = pltpu.roll(pair, 64, 1)
    a_ref[...] = scratch[ka]
    g_ref[...] = folded_gram(a)
    c = c_ref[...]
    highs, lows = [], []
    for k in range(8):
        high, low = split(a * c[:, k : k + 1])
        highs.append(high)
        lows.append(low)
    left = jnp.concatenate([jnp.concatenate(highs, axis=1), jnp.concatenate(lows, axis=1)], axis=0)
    both = jnp.dot(left, t_ref[...].reshape(4096, 512), preferred_element_type=F32)
    out = both[:RANK] + both[RANK:]
    low_lanes = low_lanes[:16]
    for q in range(4):
        pair = out[:, 128 * q : 128 * q + 128]
        turned = pltpu.roll(pair, 64, 1)
        even = jnp.where(low_lanes, pair[:16], turned[16:])
        odd = jnp.where(low_lanes, turned[:16], pair[16:])
        for ia in range(4):
            w_ref[8 * ia + 2 * q] = even
            w_ref[8 * ia + 2 * q + 1] = odd


def invert_b_kernel(
    total_i, g0_ref, g1_ref, g2_ref, g3_ref, gram_c_ref, a_ref, inv_ref, scale_ref, out_ref
):
    ja = lax.axis_index("ja")
    gram = unfold((g0_ref[...] + g1_ref[...]) + (g2_ref[...] + g3_ref[...]))
    diag = jnp.where(iota(gram.shape, 0) == iota(gram.shape, 1), gram, 0.0)
    scale_col = 1.0 / jnp.sqrt(jnp.sum(diag, axis=1, keepdims=True) / total_i + EPS)
    scale_row = 1.0 / jnp.sqrt(jnp.sum(diag, axis=0, keepdims=True) / total_i + EPS)
    inv_ref[...] = inverse(gram * scale_col * scale_row * gram_c_ref[...])
    scale_ref[...] = jnp.broadcast_to(scale_col, (RANK, LANES))
    out_ref[...] = pltpu.roll(a_ref[...] * scale_col, 32 - 4 * ja, 0)[:4, :64]


def second_solve_kernel(w_ref, inv_ref, scale_ref, raw_ref, ss_ref):
    s = total(w_ref)
    m = jnp.concatenate([s, pltpu.roll(s, 64, 1)], axis=0) * scale_ref[...]
    raw = jnp.dot(inv_ref[...], m, precision=HIGH, preferred_element_type=F32)
    raw_ref[...] = raw
    square = jnp.where(iota(raw.shape, 1) < 64, raw * raw, 0.0)
    ss = jnp.sum(square, axis=1, keepdims=True)
    eye = iota((RANK, LANES), 0) == iota((RANK, LANES), 1)
    ss_row = jnp.sum(jnp.where(eye, ss, 0.0), axis=0, keepdims=True)
    ss_ref[...] = jnp.broadcast_to(ss_row, ss_ref.shape)


def finish_kernel(total_j, ss_ref, raw_ref, out_ref):
    ia = lax.axis_index("ia")
    ss_row = jnp.sum(ss_ref[...], axis=0, keepdims=True)
    eye = iota((RANK, LANES), 0) == iota((RANK, LANES), 1)
    ss = jnp.sum(jnp.where(eye, ss_row, 0.0), axis=1, keepdims=True)
    b = raw_ref[...] / jnp.sqrt(ss / total_j + EPS)
    out_ref[...] = pltpu.roll(b, 32 - 8 * ia, 0)[:8, :64]


def call(kernel, outs, *args, scratch=(), cost=None, space=VMEM):
    return pl.pallas_call(
        kernel,
        out_shape=[jax.ShapeDtypeStruct(s, F32) for s in outs],
        in_specs=[space] * len(args),
        out_specs=[VMEM] * len(outs),
        scratch_shapes=scratch,
        cost_estimate=cost,
        compiler_params=pltpu.CompilerParams(vmem_limit_bytes=32 * 1024 * 1024),
    )(*args)


def exchange(x, axes, groups=None):
    return lax.all_to_all(x, axes, 0, 0, tiled=True, axis_index_groups=groups)


def other_core(x):
    return lax.ppermute(x, "ja", [(n, n ^ 1) for n in range(8)])


def turned(x, axis, step):
    size = lax.axis_size(axis)
    return lax.ppermute(x, axis, [(n, (n + step) % size) for n in range(size)])


def body(tensor, factor_b, factor_c):
    total_i = tensor.shape[1] * lax.axis_size("ia")
    total_j = tensor.shape[2] * lax.axis_size("ja")
    factor_b, factor_c = (
        pltpu.with_memory_space_constraint(a, pltpu.HBM) for a in (factor_b, factor_c)
    )
    (y,) = call(
        start_kernel,
        [(32, 8, LANES)],
        factor_b,
        factor_c,
        scratch=[
            pltpu.VMEM(factor_b.shape, F32),
            pltpu.VMEM(factor_c.shape, F32),
            pltpu.SemaphoreType.DMA((2,)),
        ],
        cost=LONG,
        space=HBM,
    )
    y = exchange(y, ("ia", "ka"))
    keep, send = call(
        first_kernel,
        [(4, 160, LANES), (4, 160, LANES)],
        y,
        tensor,
        scratch=[pltpu.VMEM((2, 512, LANES), F32)],
    )
    z = keep + other_core(send)
    same_core = [[8 * ja + ka for ja in range(core, 8, 2) for ka in range(8)] for core in range(2)]
    z = exchange(z, "ja", [[0, 2, 4, 6], [1, 3, 5, 7]])
    u, gram_b, c_all, c_here = call(
        combine_kernel, [(32, 16, LANES), (RANK, RANK), (RANK, 64), (RANK, LANES)], z, cost=LONG
    )
    v = exchange(u, ("ja", "ka"), same_core)
    (m,) = call(turn_kernel, [(RANK, 256)], v)
    inv_a, gram_c = call(invert_a_kernel, [(RANK, RANK), (RANK, RANK)], gram_b, c_all)
    w, g, a = call(
        second_kernel,
        [(32, 16, LANES), (8, LANES), (RANK, LANES)],
        m,
        other_core(m),
        inv_a,
        tensor,
        c_here,
        scratch=[pltpu.VMEM((8, RANK, LANES), F32)],
    )
    w = exchange(w, ("ia", "ka"))
    inv_b, scale_a, out_a = call(
        lambda *refs: invert_b_kernel(total_i, *refs),
        [(RANK, RANK), (RANK, LANES), (4, 64)],
        g,
        *(turned(g, "ia", step) for step in (1, 2, 3)),
        gram_c,
        a,
    )
    raw_b, ss = call(second_solve_kernel, [(RANK, LANES), (64, LANES)], w, inv_b, scale_a)
    ss = exchange(ss.reshape(64, 1, LANES), ("ja", "ka")).reshape(64, LANES)
    (out_b,) = call(lambda *refs: finish_kernel(total_j, *refs), [(8, 64)], ss, raw_b)
    return out_a, out_b


def solution(mesh):
    return jax.shard_map(
        body,
        mesh=mesh,
        in_specs=(P("ka", "ia", "ja"), P("ia", ("ja", "ka")), P(("ia", "ja"), "ka")),
        out_specs=(P("ja", ("ia", "ka")), P("ia", ("ja", "ka"))),
        check_vma=False,
    )
```

```python
import jax
import jax.numpy as jnp
from jax import lax
from jax.experimental import pallas as pl
from jax.experimental.pallas import tpu as pltpu
from jax.sharding import PartitionSpec as P

EPS = 1e-06
HIGH = lax.Precision.HIGHEST
F32 = jnp.float32
RANK = 32
LANES = 128
NT = (((1,), (1,)), ((), ()))
VMEM = pl.BlockSpec(memory_space=pltpu.VMEM)
HBM = pl.BlockSpec(memory_space=pltpu.HBM)
LONG = pl.CostEstimate(flops=10**10, bytes_accessed=0, transcendentals=0)


def iota(shape, axis):
    return lax.broadcasted_iota(jnp.int32, shape, axis)


def dot_nt(left, right):
    return lax.dot_general(left, right, NT, precision=HIGH, preferred_element_type=F32)


def split(x):
    high = x.astype(jnp.bfloat16)
    return high, (x - high.astype(F32)).astype(jnp.bfloat16)


def fold(x):
    n = x.shape[0] // 4
    group = iota((n, LANES), 1) // 32
    out = x[:n]
    for q in range(1, 4):
        out = jnp.where(group == q, x[n * q : n * q + n], out)
    return out


def unfold(x):
    parts = [x] + [pltpu.roll(x, LANES - 32 * q, 1) for q in range(1, 4)]
    return jnp.concatenate(parts, axis=0)[:, :32]


def total(ref, *index):
    out = ref[(0, *index)]
    for n in range(1, ref.shape[0]):
        out = out + ref[(n, *index)]
    return out


def folded_gram(x):
    return fold(dot_nt(x, jnp.concatenate([x] * 4, axis=0)))


def inverse(a):
    size = a.shape[0]
    rows, cols = iota(a.shape, 0), iota(a.shape, 1)
    for start in range(0, size, size // 2):
        spread = {p: jnp.broadcast_to(a[:, p : p + 1], a.shape) for p in range(start, start + size // 2)}
        for p in range(start, start + size // 2):
            col = spread.pop(p)
            scale = 1.0 / col[p : p + 1, :]
            row = jnp.where(cols[:1] == p, 1.0, a[p : p + 1, :]) * scale
            a = jnp.where(cols == p, 0.0, a) - col * row
            a = jnp.where(rows == p, row, a)
            for q, other in spread.items():
                there = other[p : p + 1, :] * scale
                spread[q] = jnp.where(rows == p, there, other - col * there)
    return a


def start_kernel(b_hbm, c_hbm, y_ref, b_ref, c_ref, sems):
    copies = [
        pltpu.make_async_copy(b_hbm, b_ref, sems.at[0]),
        pltpu.make_async_copy(c_hbm, c_ref, sems.at[1]),
    ]
    for copy in copies:
        copy.start()
    for copy in copies:
        copy.wait()
    ja, ka = lax.axis_index("ja"), lax.axis_index("ka")
    row, lane = iota((8, LANES), 0), iota((8, LANES), 1)
    c_tiled = jnp.concatenate([c_ref[...]] * 16, axis=1)
    c_placed = jnp.where((row == ja) & (lane // 8 == 8 + ka), c_tiled, 0.0)
    b_wide = jnp.concatenate([b_ref[...], jnp.zeros((8, 64), F32)], axis=1)
    tile = jnp.where(lane < 64, b_wide, c_placed)
    for n in range(32):
        y_ref[n] = tile


def first_kernel(other, y_ref, t_ref, *refs):
    out_ref, extra_ref = refs if other else refs[::-1]
    ja = lax.axis_index("ja")
    lane = iota((8, LANES), 1)
    b_rows, c_rows = [], []
    for ia in range(4):
        parts = [y_ref[8 * ia + ka] for ka in range(8)]
        pairs = [
            jnp.where(lane < 64, parts[2 * q], pltpu.roll(parts[2 * q + 1], 64, 1))
            for q in range(4)
        ]
        b_rows.append(jnp.concatenate(pairs, axis=1))
        c_rows.append(sum(parts[1:], parts[0]))
    b = jnp.concatenate(b_rows, axis=0)
    if other:
        c = jnp.concatenate(c_rows, axis=0)
        gram = dot_nt(b, jnp.concatenate([b, jnp.zeros((96, 512), F32)], axis=0))
        extra_ref[...] = jnp.where(iota((32, LANES), 1) < 64, gram, c)
    extra = extra_ref[...]
    high, low = split(b)

    def placed(part, q):
        zeros = jnp.zeros((RANK, 512), jnp.bfloat16)
        return [part if n == q else zeros for n in range(4)]

    weights = jnp.concatenate(
        [jnp.concatenate(placed(high, q) + placed(low, q), axis=0) for q in range(4)], axis=1
    )
    core = 1 - ja % 2 if other else ja % 2
    starts = [pl.multiple_of(64 * (2 * ((ja // 2 + n) % 4) + core), 64) for n in range(4)]
    for h in range(2):
        left = jnp.concatenate(
            [
                jnp.concatenate([t_ref[4 * h + q, pl.ds(start, 64), :] for start in starts], axis=0)
                for q in range(4)
            ],
            axis=1,
        )
        both = lax.dot_general(left, weights, NT, preferred_element_type=F32)
        y = both[:, :LANES] + both[:, LANES:]
        for n in range(4):
            out_ref[n, 64 * h : 64 * h + 64, :] = y[64 * n : 64 * n + 64]
    for n in range(4):
        out_ref[n, 128:160, :] = extra


def combine_kernel(z0_ref, z1_ref, z2_ref, z3_ref, u_ref, gram_ref, c_all_ref, c_ref):
    ka = lax.axis_index("ka")
    z = (z0_ref[...] + z1_ref[...]) + (z2_ref[...] + z3_ref[...])
    extra = z[128:160]
    gram_ref[...] = extra[:, :32]
    c_all_ref[...] = pltpu.roll(extra, 64, 1)[:, :64]
    c_here = pltpu.roll(extra, 64 - 8 * ka, 1)
    c_ref[...] = c_here
    c_t = c_here.T[:8]
    c_tiled = jnp.concatenate([c_t] * 4, axis=1)
    which = iota((8, LANES), 0) - iota((8, LANES), 1) // 32
    acc = None
    for h in range(2):
        weight = jnp.sum(jnp.where(which == 4 * h, c_tiled, 0.0), axis=0, keepdims=True)
        term = z[64 * h : 64 * h + 64] * weight
        acc = term if acc is None else acc + term
    acc = acc + pltpu.roll(acc, 64, 1)
    acc = acc + pltpu.roll(acc, 32, 1)
    u = fold(acc)
    for n in range(32):
        u_ref[n] = u


def invert_a_kernel(gram_b_ref, c_all_ref, inv_ref, gram_c_ref):
    gram_c = dot_nt(c_all_ref[...], c_all_ref[...])
    gram_c_ref[...] = gram_c
    inv_ref[...] = inverse(gram_b_ref[...] * gram_c)


def turn_kernel(v_ref, m_ref):
    parts = []
    for y in range(4):
        part = v_ref[8 * y]
        for ka in range(1, 8):
            part = part + v_ref[8 * y + ka]
        parts.append(unfold(part))
    m_ref[...] = jnp.concatenate(parts, axis=0).T


def second_kernel(
    mine_ref, other_ref, inv_ref, t_ref, c_ref, p0_ref, p1_ref, p2_ref, p3_ref, a_ref, scratch, quarters
):
    ia, ka, core = lax.axis_index("ia"), lax.axis_index("ka"), lax.axis_index("ja") % 2
    low_lanes = iota((RANK, LANES), 1) < 64
    even = jnp.where(core == 0, mine_ref[...], other_ref[...])
    odd = jnp.where(core == 0, other_ref[...], mine_ref[...])
    parts = []
    for p in range(2):
        one, two = even[:, 128 * p : 128 * p + 128], odd[:, 128 * p : 128 * p + 128]
        parts.append(jnp.where(low_lanes, one, pltpu.roll(two, 64, 1)))
        parts.append(jnp.where(low_lanes, pltpu.roll(one, 64, 1), two))
    m = jnp.concatenate(parts, axis=1)
    a = jnp.dot(inv_ref[...], m, precision=HIGH, preferred_element_type=F32)
    for q in range(4):
        pair = a[:, 128 * q : 128 * q + 128]
        scratch[2 * q] = pair
        scratch[2 * q + 1] = pltpu.roll(pair, 64, 1)
    a_ref[...] = scratch[ka]
    gram = folded_gram(a)
    c = c_ref[...]
    highs, lows = [], []
    for k in range(8):
        high, low = split(a * c[:, k : k + 1])
        highs.append(high)
        lows.append(low)
    left = jnp.concatenate([jnp.concatenate(highs, axis=1), jnp.concatenate(lows, axis=1)], axis=0)
    both = jnp.dot(left, t_ref[...].reshape(4096, 512), preferred_element_type=F32)
    out = both[:RANK] + both[RANK:]
    for q in range(4):
        quarters[q] = out[:, 128 * q : 128 * q + 128]
    for n, ref in enumerate((p0_ref, p1_ref, p2_ref, p3_ref)):
        ref[:RANK] = quarters[(ia + n) % 4]
        ref[RANK:] = gram


def sum_kernel(p0_ref, p1_ref, p2_ref, p3_ref, u_ref, gram_ref):
    p = (p0_ref[...] + p1_ref[...]) + (p2_ref[...] + p3_ref[...])
    for n in range(8):
        u_ref[n] = p[:RANK]
    gram_ref[...] = p[RANK:]


def second_solve_kernel(total_i, u_ref, gram_ref, gram_c_ref, ss_ref, scale_ref):
    half = lax.axis_index("ka") % 2
    gram = unfold(gram_ref[...])
    diag = jnp.where(iota(gram.shape, 0) == iota(gram.shape, 1), gram, 0.0)
    scale_col = 1.0 / jnp.sqrt(jnp.sum(diag, axis=1, keepdims=True) / total_i + EPS)
    scale_row = 1.0 / jnp.sqrt(jnp.sum(diag, axis=0, keepdims=True) / total_i + EPS)
    inv = inverse(gram * scale_col * scale_row * gram_c_ref[...])
    scale_ref[...] = jnp.broadcast_to(scale_col, (RANK, LANES))
    m = total(u_ref) * scale_col
    raw = jnp.dot(inv, m, precision=HIGH, preferred_element_type=F32)
    ss = jnp.sum(raw * raw, axis=1, keepdims=True)
    place = iota((RANK, LANES), 0) + 64 == iota((RANK, LANES), 1)
    ss_row = jnp.sum(jnp.where(place, ss, 0.0), axis=0, keepdims=True)
    raw = jnp.where(half == 0, raw, pltpu.roll(raw, 64, 1))
    tile = jnp.where(iota((RANK, LANES), 1) < 64, raw, ss_row)
    for n in range(32):
        ia = n // 8
        ss_ref[n] = tile[8 * ia : 8 * ia + 8]


def finish_kernel(total_j, ss_ref, a_ref, scale_ref, out_a_ref, out_b_ref):
    ia, ja, ka = lax.axis_index("ia"), lax.axis_index("ja"), lax.axis_index("ka")
    place = iota((8, LANES), 1) == iota((8, LANES), 0) + (64 + 8 * ia)
    ss = jnp.sum(jnp.where(place, total(ss_ref), 0.0), axis=1, keepdims=True)
    b = ss_ref[8 * (ka // 2) + ja] / jnp.sqrt(ss / total_j + EPS)
    out_b_ref[...] = b[:, :64]
    out_a_ref[...] = pltpu.roll(a_ref[...] * scale_ref[...], 32 - 4 * ja, 0)[:4, :64]


def call(kernel, outs, *args, scratch=(), cost=None, space=VMEM):
    return pl.pallas_call(
        kernel,
        out_shape=[jax.ShapeDtypeStruct(s, F32) for s in outs],
        in_specs=[space] * len(args),
        out_specs=[VMEM] * len(outs),
        scratch_shapes=scratch,
        cost_estimate=cost,
        compiler_params=pltpu.CompilerParams(vmem_limit_bytes=32 * 1024 * 1024),
    )(*args)


def exchange(x, axes, groups=None):
    return lax.all_to_all(x, axes, 0, 0, tiled=True, axis_index_groups=groups)


def other_core(x):
    return lax.ppermute(x, "ja", [(n, n ^ 1) for n in range(8)])


def turned(x, axis, step):
    size = lax.axis_size(axis)
    return lax.ppermute(x, axis, [(n, (n + step) % size) for n in range(size)])


def body(tensor, factor_b, factor_c):
    total_i = tensor.shape[1] * lax.axis_size("ia")
    total_j = tensor.shape[2] * lax.axis_size("ja")
    factor_b, factor_c = (
        pltpu.with_memory_space_constraint(a, pltpu.HBM) for a in (factor_b, factor_c)
    )
    (y,) = call(
        start_kernel,
        [(32, 8, LANES)],
        factor_b,
        factor_c,
        scratch=[
            pltpu.VMEM(factor_b.shape, F32),
            pltpu.VMEM(factor_c.shape, F32),
            pltpu.SemaphoreType.DMA((2,)),
        ],
        cost=LONG,
        space=HBM,
    )
    y = exchange(y, ("ia", "ka"))
    half = (4, 160, LANES)
    send, extra = call(
        lambda *refs: first_kernel(True, *refs), [half, (RANK, LANES)], y, tensor
    )
    received = other_core(send)
    (keep,) = call(lambda *refs: first_kernel(False, *refs), [half], y, tensor, extra)
    z = [keep[n] + received[n] for n in range(4)]
    z = [z[0]] + [turned(z[n], "ja", 2 * n) for n in range(1, 4)]
    same_core = [[8 * ja + ka for ja in range(core, 8, 2) for ka in range(8)] for core in range(2)]
    u, gram_b, c_all, c_here = call(
        combine_kernel, [(32, 16, LANES), (RANK, RANK), (RANK, 64), (RANK, LANES)], *z, cost=LONG
    )
    v = exchange(u, ("ja", "ka"), same_core)
    (m,) = call(turn_kernel, [(RANK, 256)], v)
    inv_a, gram_c = call(invert_a_kernel, [(RANK, RANK), (RANK, RANK)], gram_b, c_all)
    *p, a = call(
        second_kernel,
        [(40, LANES)] * 4 + [(RANK, LANES)],
        m,
        other_core(m),
        inv_a,
        tensor,
        c_here,
        scratch=[pltpu.VMEM((8, RANK, LANES), F32), pltpu.VMEM((4, RANK, LANES), F32)],
    )
    p = [p[0]] + [turned(p[n], "ia", n) for n in range(1, 4)]
    u, gram_a = call(sum_kernel, [(8, RANK, LANES), (8, LANES)], *p)
    u = exchange(u, "ka")
    ss, scale_a = call(
        lambda *refs: second_solve_kernel(total_i, *refs),
        [(32, 8, LANES), (RANK, LANES)],
        u,
        gram_a,
        gram_c,
    )
    ss = exchange(ss, ("ia", "ja"))
    out_a, out_b = call(
        lambda *refs: finish_kernel(total_j, *refs), [(4, 64), (8, 64)], ss, a, scale_a
    )
    return out_a, out_b


def solution(mesh):
    return jax.shard_map(
        body,
        mesh=mesh,
        in_specs=(P("ka", "ia", "ja"), P("ia", ("ja", "ka")), P(("ia", "ja"), "ka")),
        out_specs=(P("ja", ("ia", "ka")), P("ia", ("ja", "ka"))),
        check_vma=False,
    )
```

```python
import jax
import jax.numpy as jnp
from jax import lax
from jax.experimental import pallas as pl
from jax.experimental.pallas import tpu as pltpu
from jax.sharding import PartitionSpec as P

EPS = 1e-06
HIGH = lax.Precision.HIGHEST
F32 = jnp.float32
RANK = 32
LANES = 128
NT = (((1,), (1,)), ((), ()))
VMEM = pl.BlockSpec(memory_space=pltpu.VMEM)
HBM = pl.BlockSpec(memory_space=pltpu.HBM)
LONG = pl.CostEstimate(flops=10**10, bytes_accessed=0, transcendentals=0)


def iota(shape, axis):
    return lax.broadcasted_iota(jnp.int32, shape, axis)


def dot_nt(left, right):
    return lax.dot_general(left, right, NT, precision=HIGH, preferred_element_type=F32)


def split(x):
    high = x.astype(jnp.bfloat16)
    return high, (x - high.astype(F32)).astype(jnp.bfloat16)


def fold(x):
    n = x.shape[0] // 4
    group = iota((n, LANES), 1) // 32
    out = x[:n]
    for q in range(1, 4):
        out = jnp.where(group == q, x[n * q : n * q + n], out)
    return out


def unfold(x):
    parts = [x] + [pltpu.roll(x, LANES - 32 * q, 1) for q in range(1, 4)]
    return jnp.concatenate(parts, axis=0)[:, :32]


def total(ref, *index):
    out = ref[(0, *index)]
    for n in range(1, ref.shape[0]):
        out = out + ref[(n, *index)]
    return out


def folded_gram(x):
    return fold(dot_nt(x, jnp.concatenate([x] * 4, axis=0)))


def inverse(a):
    size = a.shape[0]
    rows, cols = iota(a.shape, 0), iota(a.shape, 1)
    for start in range(0, size, size // 2):
        spread = {p: jnp.broadcast_to(a[:, p : p + 1], a.shape) for p in range(start, start + size // 2)}
        for p in range(start, start + size // 2):
            col = spread.pop(p)
            scale = 1.0 / col[p : p + 1, :]
            row = jnp.where(cols[:1] == p, 1.0, a[p : p + 1, :]) * scale
            a = jnp.where(cols == p, 0.0, a) - col * row
            a = jnp.where(rows == p, row, a)
            for q, other in spread.items():
                there = other[p : p + 1, :] * scale
                spread[q] = jnp.where(rows == p, there, other - col * there)
    return a


def start_kernel(b_hbm, c_hbm, y_ref, b_ref, c_ref, sems):
    copies = [
        pltpu.make_async_copy(b_hbm, b_ref, sems.at[0]),
        pltpu.make_async_copy(c_hbm, c_ref, sems.at[1]),
    ]
    for copy in copies:
        copy.start()
    for copy in copies:
        copy.wait()
    lane = iota((1, LANES), 1)
    c_tiled = jnp.concatenate([c_ref[...]] * 16, axis=1)
    c_row = jnp.where(lane // 8 == 8 + lax.axis_index("ka"), c_tiled, 0.0)
    b_pairs = jnp.concatenate([b_ref[:4], b_ref[4:]], axis=1)
    tile = jnp.concatenate([b_pairs, c_row], axis=0)
    for n in range(32):
        y_ref[5 * n : 5 * n + 5] = tile


def first_kernel(other, y_ref, t_ref, *refs):
    out_ref, extra_ref = refs if other else refs[::-1]
    ja = lax.axis_index("ja")
    low_lanes = iota((4, LANES), 1) < 64
    b_rows = []
    for ia in range(4):
        starts = [5 * (8 * ia + ka) for ka in range(8)]
        parts = [y_ref[start : start + 4] for start in starts]
        pairs = []
        for one, two in zip(parts[::2], parts[1::2]):
            top = jnp.where(low_lanes, one, pltpu.roll(two, 64, 1))
            bottom = jnp.where(low_lanes, pltpu.roll(one, 64, 1), two)
            pairs.append(jnp.concatenate([top, bottom], axis=0))
        b_rows.append(jnp.concatenate(pairs, axis=1))
    b = jnp.concatenate(b_rows, axis=0)
    if other:
        extra = dot_nt(b, jnp.concatenate([b, jnp.zeros((96, 512), F32)], axis=0))
        row, lane = iota((RANK, LANES), 0), iota((RANK, LANES), 1)
        for ia in range(4):
            starts = [5 * (8 * ia + ka) + 4 for ka in range(8)]
            c_row = sum(y_ref[start : start + 1] for start in starts)
            extra = jnp.where((lane >= 64) & (row == 8 * ia + ja), c_row, extra)
        extra_ref[...] = extra
    extra = extra_ref[...]
    high, low = split(b)

    def placed(part, q):
        zeros = jnp.zeros((RANK, 512), jnp.bfloat16)
        return [part if n == q else zeros for n in range(4)]

    weights = jnp.concatenate(
        [jnp.concatenate(placed(high, q) + placed(low, q), axis=0) for q in range(4)], axis=1
    )
    core = 1 - ja % 2 if other else ja % 2
    starts = [pl.multiple_of(64 * (2 * ((ja // 2 + n) % 4) + core), 64) for n in range(4)]
    for h in range(2):
        left = jnp.concatenate(
            [
                jnp.concatenate([t_ref[4 * h + q, pl.ds(start, 64), :] for start in starts], axis=0)
                for q in range(4)
            ],
            axis=1,
        )
        both = lax.dot_general(left, weights, NT, preferred_element_type=F32)
        y = both[:, :LANES] + both[:, LANES:]
        for n in range(4):
            out_ref[n, 64 * h : 64 * h + 64, :] = y[64 * n : 64 * n + 64]
    for n in range(4):
        out_ref[n, 128:160, :] = extra


def combine_kernel(z0_ref, z1_ref, z2_ref, z3_ref, u_ref, gram_ref, c_all_ref, c_ref):
    ka = lax.axis_index("ka")
    z = (z0_ref[...] + z1_ref[...]) + (z2_ref[...] + z3_ref[...])
    extra = z[128:160]
    gram_ref[...] = extra[:, :32]
    c_all_ref[...] = pltpu.roll(extra, 64, 1)[:, :64]
    c_here = pltpu.roll(extra, 64 - 8 * ka, 1)
    c_ref[...] = c_here
    c_t = c_here.T[:8]
    c_tiled = jnp.concatenate([c_t] * 4, axis=1)
    which = iota((8, LANES), 0) - iota((8, LANES), 1) // 32
    acc = None
    for h in range(2):
        weight = jnp.sum(jnp.where(which == 4 * h, c_tiled, 0.0), axis=0, keepdims=True)
        term = z[64 * h : 64 * h + 64] * weight
        acc = term if acc is None else acc + term
    acc = acc + pltpu.roll(acc, 64, 1)
    acc = acc + pltpu.roll(acc, 32, 1)
    u = fold(acc)
    for n in range(32):
        u_ref[n] = u


def invert_a_kernel(gram_b_ref, c_all_ref, inv_ref, gram_c_ref):
    gram_c = dot_nt(c_all_ref[...], c_all_ref[...])
    gram_c_ref[...] = gram_c
    inv_ref[...] = inverse(gram_b_ref[...] * gram_c)


def turn_kernel(v_ref, m_ref):
    parts = []
    for y in range(4):
        part = v_ref[8 * y]
        for ka in range(1, 8):
            part = part + v_ref[8 * y + ka]
        parts.append(unfold(part))
    m_ref[...] = jnp.concatenate(parts, axis=0).T


def second_kernel(
    mine_ref, other_ref, inv_ref, t_ref, c_ref, p0_ref, p1_ref, p2_ref, p3_ref, a_ref, scratch, quarters
):
    ia, ka, core = lax.axis_index("ia"), lax.axis_index("ka"), lax.axis_index("ja") % 2
    low_lanes = iota((RANK, LANES), 1) < 64
    even = jnp.where(core == 0, mine_ref[...], other_ref[...])
    odd = jnp.where(core == 0, other_ref[...], mine_ref[...])
    parts = []
    for p in range(2):
        one, two = even[:, 128 * p : 128 * p + 128], odd[:, 128 * p : 128 * p + 128]
        parts.append(jnp.where(low_lanes, one, pltpu.roll(two, 64, 1)))
        parts.append(jnp.where(low_lanes, pltpu.roll(one, 64, 1), two))
    m = jnp.concatenate(parts, axis=1)
    a = jnp.dot(inv_ref[...], m, precision=HIGH, preferred_element_type=F32)
    for q in range(4):
        pair = a[:, 128 * q : 128 * q + 128]
        scratch[2 * q] = pair
        scratch[2 * q + 1] = pltpu.roll(pair, 64, 1)
    a_ref[...] = scratch[ka]
    gram = folded_gram(a)
    c = c_ref[...]
    highs, lows = [], []
    for k in range(8):
        high, low = split(a * c[:, k : k + 1])
        highs.append(high)
        lows.append(low)
    left = jnp.concatenate([jnp.concatenate(highs, axis=1), jnp.concatenate(lows, axis=1)], axis=0)
    both = jnp.dot(left, t_ref[...].reshape(4096, 512), preferred_element_type=F32)
    out = both[:RANK] + both[RANK:]
    for q in range(4):
        quarters[q] = out[:, 128 * q : 128 * q + 128]
    for n, ref in enumerate((p0_ref, p1_ref, p2_ref, p3_ref)):
        ref[:RANK] = quarters[(ia + n) % 4]
        ref[RANK:] = gram


def sum_kernel(p0_ref, p1_ref, p2_ref, p3_ref, u_ref, gram_ref):
    p = (p0_ref[...] + p1_ref[...]) + (p2_ref[...] + p3_ref[...])
    for n in range(8):
        u_ref[n] = p[:RANK]
    gram_ref[...] = p[RANK:]


def second_solve_kernel(total_i, u_ref, gram_ref, gram_c_ref, ss_ref, scale_ref):
    half = lax.axis_index("ka") % 2
    gram = unfold(gram_ref[...])
    diag = jnp.where(iota(gram.shape, 0) == iota(gram.shape, 1), gram, 0.0)
    scale_col = 1.0 / jnp.sqrt(jnp.sum(diag, axis=1, keepdims=True) / total_i + EPS)
    scale_row = 1.0 / jnp.sqrt(jnp.sum(diag, axis=0, keepdims=True) / total_i + EPS)
    inv = inverse(gram * scale_col * scale_row * gram_c_ref[...])
    scale_ref[...] = jnp.broadcast_to(scale_col, (RANK, LANES))
    m = total(u_ref) * scale_col
    raw = jnp.dot(inv, m, precision=HIGH, preferred_element_type=F32)
    ss = jnp.sum(raw * raw, axis=1, keepdims=True)
    place = iota((RANK, LANES), 0) == iota((RANK, LANES), 1)
    ss_row = jnp.sum(jnp.where(place, ss, 0.0), axis=0, keepdims=True)
    raw = jnp.where(half == 0, raw, pltpu.roll(raw, 64, 1))
    turned_raw = pltpu.roll(raw, 64, 1)
    low_lanes = iota((4, LANES), 1) < 64
    for ia in range(4):
        data = jnp.where(low_lanes, raw[8 * ia : 8 * ia + 4], turned_raw[8 * ia + 4 : 8 * ia + 8])
        tile = jnp.concatenate([data, ss_row], axis=0)
        for ja in range(8):
            start = 5 * (8 * ia + ja)
            ss_ref[start : start + 5] = tile


def finish_kernel(total_j, ss_ref, a_ref, scale_ref, out_a_ref, out_b_ref):
    ia, ja, ka = lax.axis_index("ia"), lax.axis_index("ja"), lax.axis_index("ka")
    place = iota((8, LANES), 1) == iota((8, LANES), 0) + 8 * ia
    ss_row = jnp.sum(ss_ref[pl.ds(4, 32, stride=5), :], axis=0, keepdims=True)
    ss = jnp.sum(jnp.where(place, ss_row, 0.0), axis=1, keepdims=True)
    data = ss_ref[pl.ds(5 * (8 * (ka // 2) + ja), 4), :]
    b = jnp.concatenate([data, pltpu.roll(data, 64, 1)], axis=0) / jnp.sqrt(ss / total_j + EPS)
    out_b_ref[...] = b[:, :64]
    out_a_ref[...] = pltpu.roll(a_ref[...] * scale_ref[...], (32 - 4 * ja) % 32, 0)[:4, :64]


def call(kernel, outs, *args, scratch=(), cost=None, space=VMEM):
    return pl.pallas_call(
        kernel,
        out_shape=[jax.ShapeDtypeStruct(s, F32) for s in outs],
        in_specs=[space] * len(args),
        out_specs=[VMEM] * len(outs),
        scratch_shapes=scratch,
        cost_estimate=cost,
        compiler_params=pltpu.CompilerParams(vmem_limit_bytes=32 * 1024 * 1024),
    )(*args)


def exchange(x, axes, groups=None):
    return lax.all_to_all(x, axes, 0, 0, tiled=True, axis_index_groups=groups)


def other_core(x):
    return lax.ppermute(x, "ja", [(n, n ^ 1) for n in range(8)])


def turned(x, axis, step):
    size = lax.axis_size(axis)
    return lax.ppermute(x, axis, [(n, (n + step) % size) for n in range(size)])


def body(tensor, factor_b, factor_c):
    total_i = tensor.shape[1] * lax.axis_size("ia")
    total_j = tensor.shape[2] * lax.axis_size("ja")
    factor_b, factor_c = (
        pltpu.with_memory_space_constraint(a, pltpu.HBM) for a in (factor_b, factor_c)
    )
    (y,) = call(
        start_kernel,
        [(160, LANES)],
        factor_b,
        factor_c,
        scratch=[
            pltpu.VMEM(factor_b.shape, F32),
            pltpu.VMEM(factor_c.shape, F32),
            pltpu.SemaphoreType.DMA((2,)),
        ],
        cost=LONG,
        space=HBM,
    )
    y = exchange(y.reshape(32, 1, 5 * LANES), ("ia", "ka")).reshape(160, LANES)
    half = (4, 160, LANES)
    send, extra = call(
        lambda *refs: first_kernel(True, *refs), [half, (RANK, LANES)], y, tensor
    )
    received = other_core(send)
    (keep,) = call(lambda *refs: first_kernel(False, *refs), [half], y, tensor, extra)
    z = [keep[n] + received[n] for n in range(4)]
    z = [z[0]] + [turned(z[n], "ja", 2 * n) for n in range(1, 4)]
    same_core = [[8 * ja + ka for ja in range(core, 8, 2) for ka in range(8)] for core in range(2)]
    u, gram_b, c_all, c_here = call(
        combine_kernel, [(32, 16, LANES), (RANK, RANK), (RANK, 64), (RANK, LANES)], *z, cost=LONG
    )
    v = exchange(u, ("ja", "ka"), same_core)
    (m,) = call(turn_kernel, [(RANK, 256)], v)
    inv_a, gram_c = call(invert_a_kernel, [(RANK, RANK), (RANK, RANK)], gram_b, c_all)
    *p, a = call(
        second_kernel,
        [(40, LANES)] * 4 + [(RANK, LANES)],
        m,
        other_core(m),
        inv_a,
        tensor,
        c_here,
        scratch=[pltpu.VMEM((8, RANK, LANES), F32), pltpu.VMEM((4, RANK, LANES), F32)],
    )
    p = [p[0]] + [turned(p[n], "ia", n) for n in range(1, 4)]
    u, gram_a = call(sum_kernel, [(8, RANK, LANES), (8, LANES)], *p)
    u = exchange(u, "ka")
    ss, scale_a = call(
        lambda *refs: second_solve_kernel(total_i, *refs),
        [(160, LANES), (RANK, LANES)],
        u,
        gram_a,
        gram_c,
    )
    ss = exchange(ss.reshape(32, 1, 5 * LANES), ("ia", "ja")).reshape(160, LANES)
    out_a, out_b = call(
        lambda *refs: finish_kernel(total_j, *refs), [(4, 64), (8, 64)], ss, a, scale_a
    )
    return out_a, out_b


def solution(mesh):
    return jax.shard_map(
        body,
        mesh=mesh,
        in_specs=(P("ka", "ia", "ja"), P("ia", ("ja", "ka")), P(("ia", "ja"), "ka")),
        out_specs=(P("ja", ("ia", "ka")), P("ia", ("ja", "ka"))),
        check_vma=False,
    )
```

```python
import jax
import jax.numpy as jnp
from jax import lax
from jax.experimental import pallas as pl
from jax.experimental.pallas import tpu as pltpu
from jax.sharding import PartitionSpec as P

EPS = 1e-06
HIGH = lax.Precision.HIGHEST
F32 = jnp.float32
RANK = 32
LANES = 128
NT = (((1,), (1,)), ((), ()))
VMEM = pl.BlockSpec(memory_space=pltpu.VMEM)
HBM = pl.BlockSpec(memory_space=pltpu.HBM)
LONG = pl.CostEstimate(flops=10**10, bytes_accessed=0, transcendentals=0)


def iota(shape, axis):
    return lax.broadcasted_iota(jnp.int32, shape, axis)


def dot_nt(left, right):
    return lax.dot_general(left, right, NT, precision=HIGH, preferred_element_type=F32)


def split(x):
    high = x.astype(jnp.bfloat16)
    return high, (x - high.astype(F32)).astype(jnp.bfloat16)


def fold(x):
    n = x.shape[0] // 4
    group = iota((n, LANES), 1) // 32
    out = x[:n]
    for q in range(1, 4):
        out = jnp.where(group == q, x[n * q : n * q + n], out)
    return out


def unfold(x):
    parts = [x] + [pltpu.roll(x, LANES - 32 * q, 1) for q in range(1, 4)]
    return jnp.concatenate(parts, axis=0)[:, :32]


def total(ref, *index):
    out = ref[(0, *index)]
    for n in range(1, ref.shape[0]):
        out = out + ref[(n, *index)]
    return out


def folded_gram(x):
    return fold(dot_nt(x, jnp.concatenate([x] * 4, axis=0)))


def inverse(a):
    size = a.shape[0]
    rows, cols = iota(a.shape, 0), iota(a.shape, 1)
    for start in range(0, size, size // 2):
        spread = {p: jnp.broadcast_to(a[:, p : p + 1], a.shape) for p in range(start, start + size // 2)}
        for p in range(start, start + size // 2):
            col = spread.pop(p)
            scale = 1.0 / col[p : p + 1, :]
            row = jnp.where(cols[:1] == p, 1.0, a[p : p + 1, :]) * scale
            a = jnp.where(cols == p, 0.0, a) - col * row
            a = jnp.where(rows == p, row, a)
            for q, other in spread.items():
                there = other[p : p + 1, :] * scale
                spread[q] = jnp.where(rows == p, there, other - col * there)
    return a


def start_kernel(b_hbm, c_hbm, y_ref, b_ref, c_ref, sems):
    copies = [
        pltpu.make_async_copy(b_hbm, b_ref, sems.at[0]),
        pltpu.make_async_copy(c_hbm, c_ref, sems.at[1]),
    ]
    for copy in copies:
        copy.start()
    for copy in copies:
        copy.wait()
    lane = iota((1, LANES), 1)
    c_tiled = jnp.concatenate([c_ref[...]] * 16, axis=1)
    c_row = jnp.where(lane // 8 == 8 + lax.axis_index("ka"), c_tiled, 0.0)
    b_pairs = jnp.concatenate([b_ref[:4], b_ref[4:]], axis=1)
    tile = jnp.concatenate([b_pairs, c_row], axis=0)
    for n in range(32):
        y_ref[5 * n : 5 * n + 5] = tile


def first_kernel(other, y_ref, t_ref, *refs):
    out_ref, extra_ref = refs if other else refs[::-1]
    ja = lax.axis_index("ja")
    low_lanes = iota((4, LANES), 1) < 64
    b_rows = []
    for ia in range(4):
        starts = [5 * (8 * ia + ka) for ka in range(8)]
        parts = [y_ref[start : start + 4] for start in starts]
        pairs = []
        for one, two in zip(parts[::2], parts[1::2]):
            top = jnp.where(low_lanes, one, pltpu.roll(two, 64, 1))
            bottom = jnp.where(low_lanes, pltpu.roll(one, 64, 1), two)
            pairs.append(jnp.concatenate([top, bottom], axis=0))
        b_rows.append(jnp.concatenate(pairs, axis=1))
    b = jnp.concatenate(b_rows, axis=0)
    if other:
        extra_ref[:8] = folded_gram(b)
        row = iota((8, LANES), 0)
        c_rows = jnp.zeros((8, LANES), F32)
        for ia in range(4):
            starts = [5 * (8 * ia + ka) + 4 for ka in range(8)]
            c_row = sum(y_ref[start : start + 1] for start in starts)
            c_rows = jnp.where(row == 4 * (ja % 2) + ia, c_row, c_rows)
        extra_ref[8:] = c_rows
    extra = extra_ref[...]
    high, low = split(b)

    def placed(part, q):
        zeros = jnp.zeros((RANK, 512), jnp.bfloat16)
        return [part if n == q else zeros for n in range(4)]

    weights = jnp.concatenate(
        [jnp.concatenate(placed(high, q) + placed(low, q), axis=0) for q in range(4)], axis=1
    )
    core = 1 - ja % 2 if other else ja % 2
    starts = [pl.multiple_of(64 * (2 * ((ja // 2 + n) % 4) + core), 64) for n in range(4)]
    for h in range(2):
        left = jnp.concatenate(
            [
                jnp.concatenate([t_ref[4 * h + q, pl.ds(start, 64), :] for start in starts], axis=0)
                for q in range(4)
            ],
            axis=1,
        )
        both = lax.dot_general(left, weights, NT, preferred_element_type=F32)
        y = both[:, :LANES] + both[:, LANES:]
        for n in range(4):
            out_ref[n, 64 * h : 64 * h + 64, :] = y[64 * n : 64 * n + 64]
    for n in range(4):
        out_ref[n, 128:144, :] = extra


def combine_kernel(z0_ref, z1_ref, z2_ref, z3_ref, u_ref, gram_ref, c_all_ref, c_ref, scratch):
    ka, y = lax.axis_index("ka"), lax.axis_index("ja") // 2
    for n, ref in enumerate((z0_ref, z1_ref, z2_ref, z3_ref)):
        for core in range(2):
            place = pl.ds(2 * ((y + 4 - n) % 4) + core, 4, stride=8)
            scratch[place, :] = ref[136 + 4 * core : 140 + 4 * core]
    extra = scratch[...]
    z = (z0_ref[...] + z1_ref[...]) + (z2_ref[...] + z3_ref[...])
    gram_ref[...] = unfold(z[128:136])
    c_all_ref[...] = pltpu.roll(extra, 64, 1)[:, :64]
    c_here = pltpu.roll(extra, 64 - 8 * ka, 1)
    c_ref[...] = c_here
    c_t = c_here.T[:8]
    c_tiled = jnp.concatenate([c_t] * 4, axis=1)
    which = iota((8, LANES), 0) - iota((8, LANES), 1) // 32
    acc = None
    for h in range(2):
        weight = jnp.sum(jnp.where(which == 4 * h, c_tiled, 0.0), axis=0, keepdims=True)
        term = z[64 * h : 64 * h + 64] * weight
        acc = term if acc is None else acc + term
    acc = acc + pltpu.roll(acc, 64, 1)
    acc = acc + pltpu.roll(acc, 32, 1)
    u = fold(acc)
    for n in range(32):
        u_ref[n] = u


def invert_a_kernel(gram_b_ref, c_all_ref, inv_ref, gram_c_ref):
    gram_c = dot_nt(c_all_ref[...], c_all_ref[...])
    gram_c_ref[...] = gram_c
    inv_ref[...] = inverse(gram_b_ref[...] * gram_c)


def turn_kernel(v_ref, m_ref):
    parts = []
    for y in range(4):
        part = v_ref[8 * y]
        for ka in range(1, 8):
            part = part + v_ref[8 * y + ka]
        parts.append(unfold(part))
    m_ref[...] = jnp.concatenate(parts, axis=0).T


def second_kernel(
    mine_ref, other_ref, inv_ref, t_ref, c_ref, p0_ref, p1_ref, p2_ref, p3_ref, a_ref, scratch, quarters
):
    ia, ka, core = lax.axis_index("ia"), lax.axis_index("ka"), lax.axis_index("ja") % 2
    low_lanes = iota((RANK, LANES), 1) < 64
    even = jnp.where(core == 0, mine_ref[...], other_ref[...])
    odd = jnp.where(core == 0, other_ref[...], mine_ref[...])
    parts = []
    for p in range(2):
        one, two = even[:, 128 * p : 128 * p + 128], odd[:, 128 * p : 128 * p + 128]
        parts.append(jnp.where(low_lanes, one, pltpu.roll(two, 64, 1)))
        parts.append(jnp.where(low_lanes, pltpu.roll(one, 64, 1), two))
    m = jnp.concatenate(parts, axis=1)
    a = jnp.dot(inv_ref[...], m, precision=HIGH, preferred_element_type=F32)
    for q in range(4):
        pair = a[:, 128 * q : 128 * q + 128]
        scratch[2 * q] = pair
        scratch[2 * q + 1] = pltpu.roll(pair, 64, 1)
    a_ref[...] = scratch[ka]
    gram = folded_gram(a)
    c = c_ref[...]
    highs, lows = [], []
    for k in range(8):
        high, low = split(a * c[:, k : k + 1])
        highs.append(high)
        lows.append(low)
    left = jnp.concatenate([jnp.concatenate(highs, axis=1), jnp.concatenate(lows, axis=1)], axis=0)
    both = jnp.dot(left, t_ref[...].reshape(4096, 512), preferred_element_type=F32)
    out = both[:RANK] + both[RANK:]
    for q in range(4):
        quarters[q] = out[:, 128 * q : 128 * q + 128]
    for n, ref in enumerate((p0_ref, p1_ref, p2_ref, p3_ref)):
        ref[:RANK] = quarters[(ia + n) % 4]
        ref[RANK:] = gram


def sum_kernel(p0_ref, p1_ref, p2_ref, p3_ref, u_ref, gram_ref):
    p = (p0_ref[...] + p1_ref[...]) + (p2_ref[...] + p3_ref[...])
    for n in range(8):
        u_ref[n] = p[:RANK]
    gram_ref[...] = p[RANK:]


def second_solve_kernel(total_i, u_ref, gram_ref, gram_c_ref, ss_ref, scale_ref):
    half = lax.axis_index("ka") % 2
    gram = unfold(gram_ref[...])
    diag = jnp.where(iota(gram.shape, 0) == iota(gram.shape, 1), gram, 0.0)
    scale_col = 1.0 / jnp.sqrt(jnp.sum(diag, axis=1, keepdims=True) / total_i + EPS)
    scale_row = 1.0 / jnp.sqrt(jnp.sum(diag, axis=0, keepdims=True) / total_i + EPS)
    inv = inverse(gram * scale_col * scale_row * gram_c_ref[...])
    scale_ref[...] = jnp.broadcast_to(scale_col, (RANK, LANES))
    m = total(u_ref) * scale_col
    raw = jnp.dot(inv, m, precision=HIGH, preferred_element_type=F32)
    ss = jnp.sum(raw * raw, axis=1, keepdims=True)
    place = iota((RANK, LANES), 0) == iota((RANK, LANES), 1)
    ss_row = jnp.sum(jnp.where(place, ss, 0.0), axis=0, keepdims=True)
    raw = jnp.where(half == 0, raw, pltpu.roll(raw, 64, 1))
    turned_raw = pltpu.roll(raw, 64, 1)
    low_lanes = iota((4, LANES), 1) < 64
    for ia in range(4):
        data = jnp.where(low_lanes, raw[8 * ia : 8 * ia + 4], turned_raw[8 * ia + 4 : 8 * ia + 8])
        tile = jnp.concatenate([data, ss_row], axis=0)
        for ja in range(8):
            start = 5 * (8 * ia + ja)
            ss_ref[start : start + 5] = tile


def finish_kernel(total_j, ss_ref, a_ref, scale_ref, out_a_ref, out_b_ref):
    ia, ja, ka = lax.axis_index("ia"), lax.axis_index("ja"), lax.axis_index("ka")
    place = iota((8, LANES), 1) == iota((8, LANES), 0) + 8 * ia
    ss_row = jnp.sum(ss_ref[pl.ds(4, 32, stride=5), :], axis=0, keepdims=True)
    ss = jnp.sum(jnp.where(place, ss_row, 0.0), axis=1, keepdims=True)
    data = ss_ref[pl.ds(5 * (8 * (ka // 2) + ja), 4), :]
    b = jnp.concatenate([data, pltpu.roll(data, 64, 1)], axis=0) / jnp.sqrt(ss / total_j + EPS)
    out_b_ref[...] = b[:, :64]
    out_a_ref[...] = pltpu.roll(a_ref[...] * scale_ref[...], (32 - 4 * ja) % 32, 0)[:4, :64]


def call(kernel, outs, *args, scratch=(), cost=None, space=VMEM):
    return pl.pallas_call(
        kernel,
        out_shape=[jax.ShapeDtypeStruct(s, F32) for s in outs],
        in_specs=[space] * len(args),
        out_specs=[VMEM] * len(outs),
        scratch_shapes=scratch,
        cost_estimate=cost,
        compiler_params=pltpu.CompilerParams(vmem_limit_bytes=32 * 1024 * 1024),
    )(*args)


def exchange(x, axes, groups=None):
    return lax.all_to_all(x, axes, 0, 0, tiled=True, axis_index_groups=groups)


def other_core(x):
    return lax.ppermute(x, "ja", [(n, n ^ 1) for n in range(8)])


def turned(x, axis, step):
    size = lax.axis_size(axis)
    return lax.ppermute(x, axis, [(n, (n + step) % size) for n in range(size)])


def body(tensor, factor_b, factor_c):
    total_i = tensor.shape[1] * lax.axis_size("ia")
    total_j = tensor.shape[2] * lax.axis_size("ja")
    factor_b, factor_c = (
        pltpu.with_memory_space_constraint(a, pltpu.HBM) for a in (factor_b, factor_c)
    )
    (y,) = call(
        start_kernel,
        [(160, LANES)],
        factor_b,
        factor_c,
        scratch=[
            pltpu.VMEM(factor_b.shape, F32),
            pltpu.VMEM(factor_c.shape, F32),
            pltpu.SemaphoreType.DMA((2,)),
        ],
        cost=LONG,
        space=HBM,
    )
    y = exchange(y.reshape(32, 1, 5 * LANES), ("ia", "ka")).reshape(160, LANES)
    half = (4, 144, LANES)
    send, extra = call(
        lambda *refs: first_kernel(True, *refs), [half, (16, LANES)], y, tensor
    )
    received = other_core(send)
    (keep,) = call(lambda *refs: first_kernel(False, *refs), [half], y, tensor, extra)
    z = [keep[n] + received[n] for n in range(4)]
    z = [z[0]] + [turned(z[n], "ja", 2 * n) for n in range(1, 4)]
    same_core = [[8 * ja + ka for ja in range(core, 8, 2) for ka in range(8)] for core in range(2)]
    u, gram_b, c_all, c_here = call(
        combine_kernel,
        [(32, 16, LANES), (RANK, RANK), (RANK, 64), (RANK, LANES)],
        *z,
        scratch=[pltpu.VMEM((RANK, LANES), F32)],
        cost=LONG,
    )
    v = exchange(u, ("ja", "ka"), same_core)
    (m,) = call(turn_kernel, [(RANK, 256)], v)
    inv_a, gram_c = call(invert_a_kernel, [(RANK, RANK), (RANK, RANK)], gram_b, c_all)
    *p, a = call(
        second_kernel,
        [(40, LANES)] * 4 + [(RANK, LANES)],
        m,
        other_core(m),
        inv_a,
        tensor,
        c_here,
        scratch=[pltpu.VMEM((8, RANK, LANES), F32), pltpu.VMEM((4, RANK, LANES), F32)],
    )
    p = [p[0]] + [turned(p[n], "ia", n) for n in range(1, 4)]
    u, gram_a = call(sum_kernel, [(8, RANK, LANES), (8, LANES)], *p)
    u = exchange(u, "ka")
    ss, scale_a = call(
        lambda *refs: second_solve_kernel(total_i, *refs),
        [(160, LANES), (RANK, LANES)],
        u,
        gram_a,
        gram_c,
    )
    ss = exchange(ss.reshape(32, 1, 5 * LANES), ("ia", "ja")).reshape(160, LANES)
    out_a, out_b = call(
        lambda *refs: finish_kernel(total_j, *refs), [(4, 64), (8, 64)], ss, a, scale_a
    )
    return out_a, out_b


def solution(mesh):
    return jax.shard_map(
        body,
        mesh=mesh,
        in_specs=(P("ka", "ia", "ja"), P("ia", ("ja", "ka")), P(("ia", "ja"), "ka")),
        out_specs=(P("ja", ("ia", "ka")), P("ia", ("ja", "ka"))),
        check_vma=False,
    )
```

```python
import jax
import jax.numpy as jnp
from jax import lax
from jax.experimental import pallas as pl
from jax.experimental.pallas import tpu as pltpu
from jax.sharding import PartitionSpec as P

EPS = 1e-06
HIGH = lax.Precision.HIGHEST
F32 = jnp.float32
RANK = 32
LANES = 128
NT = (((1,), (1,)), ((), ()))
VMEM = pl.BlockSpec(memory_space=pltpu.VMEM)
HBM = pl.BlockSpec(memory_space=pltpu.HBM)
LONG = pl.CostEstimate(flops=10**10, bytes_accessed=0, transcendentals=0)


def iota(shape, axis):
    return lax.broadcasted_iota(jnp.int32, shape, axis)


def dot_nt(left, right):
    return lax.dot_general(left, right, NT, precision=HIGH, preferred_element_type=F32)


def split(x):
    high = x.astype(jnp.bfloat16)
    return high, (x - high.astype(F32)).astype(jnp.bfloat16)


def fold(x):
    n = x.shape[0] // 4
    group = iota((n, LANES), 1) // 32
    out = x[:n]
    for q in range(1, 4):
        out = jnp.where(group == q, x[n * q : n * q + n], out)
    return out


def unfold(x):
    parts = [x] + [pltpu.roll(x, LANES - 32 * q, 1) for q in range(1, 4)]
    return jnp.concatenate(parts, axis=0)[:, :32]


def total(ref, *index):
    out = ref[(0, *index)]
    for n in range(1, ref.shape[0]):
        out = out + ref[(n, *index)]
    return out


def folded_gram(x):
    gram = dot_nt(x, x)
    return jnp.concatenate([gram[8 * q : 8 * q + 8] for q in range(4)], axis=1)


def inverse(a):
    size = a.shape[0]
    rows, cols = iota(a.shape, 0), iota(a.shape, 1)
    for start in range(0, size, size // 2):
        spread = {p: jnp.broadcast_to(a[:, p : p + 1], a.shape) for p in range(start, start + size // 2)}
        for p in range(start, start + size // 2):
            col = spread.pop(p)
            scale = 1.0 / col[p : p + 1, :]
            row = jnp.where(cols[:1] == p, 1.0, a[p : p + 1, :]) * scale
            a = jnp.where(cols == p, 0.0, a) - col * row
            a = jnp.where(rows == p, row, a)
            for q, other in spread.items():
                there = other[p : p + 1, :] * scale
                spread[q] = jnp.where(rows == p, there, other - col * there)
    return a


def start_kernel(b_hbm, c_hbm, y_ref, b_ref, c_ref, sems):
    copies = [
        pltpu.make_async_copy(b_hbm, b_ref, sems.at[0]),
        pltpu.make_async_copy(c_hbm, c_ref, sems.at[1]),
    ]
    for copy in copies:
        copy.start()
    for copy in copies:
        copy.wait()
    lane = iota((1, LANES), 1)
    c_tiled = jnp.concatenate([c_ref[...]] * 16, axis=1)
    c_row = jnp.where(lane // 8 == 8 + lax.axis_index("ka"), c_tiled, 0.0)
    b_pairs = jnp.concatenate([b_ref[:4], b_ref[4:]], axis=1)
    tile = jnp.concatenate([b_pairs, c_row], axis=0)
    for n in range(32):
        y_ref[5 * n : 5 * n + 5] = tile


def first_kernel(other, y_ref, t_ref, *refs):
    out_ref, extra_ref = refs if other else refs[::-1]
    ja = lax.axis_index("ja")
    low_lanes = iota((4, LANES), 1) < 64
    b_rows = []
    for ia in range(4):
        starts = [5 * (8 * ia + ka) for ka in range(8)]
        parts = [y_ref[start : start + 4] for start in starts]
        pairs = []
        for one, two in zip(parts[::2], parts[1::2]):
            top = jnp.where(low_lanes, one, pltpu.roll(two, 64, 1))
            bottom = jnp.where(low_lanes, pltpu.roll(one, 64, 1), two)
            pairs.append(jnp.concatenate([top, bottom], axis=0))
        b_rows.append(jnp.concatenate(pairs, axis=1))
    b = jnp.concatenate(b_rows, axis=0)
    if other:
        extra_ref[:8] = folded_gram(b)
        row = iota((8, LANES), 0)
        c_rows = jnp.zeros((8, LANES), F32)
        for ia in range(4):
            starts = [5 * (8 * ia + ka) + 4 for ka in range(8)]
            c_row = sum(y_ref[start : start + 1] for start in starts)
            c_rows = jnp.where(row == 4 * (ja % 2) + ia, c_row, c_rows)
        extra_ref[8:] = c_rows
    extra = extra_ref[...]
    high, low = split(b)

    def placed(part, q):
        zeros = jnp.zeros((RANK, 512), jnp.bfloat16)
        return [part if n == q else zeros for n in range(4)]

    weights = jnp.concatenate(
        [jnp.concatenate(placed(high, q) + placed(low, q), axis=0) for q in range(4)], axis=1
    )
    core = 1 - ja % 2 if other else ja % 2
    starts = [pl.multiple_of(64 * (2 * ((ja // 2 + n) % 4) + core), 64) for n in range(4)]
    for h in range(2):
        left = jnp.concatenate(
            [
                jnp.concatenate([t_ref[4 * h + q, pl.ds(start, 64), :] for start in starts], axis=0)
                for q in range(4)
            ],
            axis=1,
        )
        both = lax.dot_general(left, weights, NT, preferred_element_type=F32)
        y = both[:, :LANES] + both[:, LANES:]
        for n in range(4):
            out_ref[n, 64 * h : 64 * h + 64, :] = y[64 * n : 64 * n + 64]
    for n in range(4):
        out_ref[n, 128:144, :] = extra


def combine_kernel(z0_ref, z1_ref, z2_ref, z3_ref, u_ref, gram_ref, c_all_ref, c_ref, scratch):
    ka, y = lax.axis_index("ka"), lax.axis_index("ja") // 2
    for n, ref in enumerate((z0_ref, z1_ref, z2_ref, z3_ref)):
        for core in range(2):
            place = pl.ds(2 * ((y + 4 - n) % 4) + core, 4, stride=8)
            scratch[place, :] = ref[136 + 4 * core : 140 + 4 * core]
    extra = scratch[...]
    z = (z0_ref[...] + z1_ref[...]) + (z2_ref[...] + z3_ref[...])
    gram_ref[...] = unfold(z[128:136])
    c_all_ref[...] = pltpu.roll(extra, 64, 1)[:, :64]
    c_here = pltpu.roll(extra, 64 - 8 * ka, 1)
    c_ref[...] = c_here
    c_t = c_here.T[:8]
    c_tiled = jnp.concatenate([c_t] * 4, axis=1)
    which = iota((8, LANES), 0) - iota((8, LANES), 1) // 32
    acc = None
    for h in range(2):
        weight = jnp.sum(jnp.where(which == 4 * h, c_tiled, 0.0), axis=0, keepdims=True)
        term = z[64 * h : 64 * h + 64] * weight
        acc = term if acc is None else acc + term
    acc = acc + pltpu.roll(acc, 64, 1)
    acc = acc + pltpu.roll(acc, 32, 1)
    u = fold(acc)
    for n in range(32):
        u_ref[n] = u


def invert_a_kernel(gram_b_ref, c_all_ref, inv_ref, gram_c_ref):
    gram_c = dot_nt(c_all_ref[...], c_all_ref[...])
    gram_c_ref[...] = gram_c
    inv_ref[...] = inverse(gram_b_ref[...] * gram_c)


def turn_kernel(v_ref, m_ref):
    parts = []
    for y in range(4):
        part = v_ref[8 * y]
        for ka in range(1, 8):
            part = part + v_ref[8 * y + ka]
        parts.append(unfold(part))
    m_ref[...] = jnp.concatenate(parts, axis=0).T


def second_kernel(
    mine_ref, other_ref, inv_ref, t_ref, c_ref, p0_ref, p1_ref, p2_ref, p3_ref, a_ref, scratch, quarters
):
    ia, ka, core = lax.axis_index("ia"), lax.axis_index("ka"), lax.axis_index("ja") % 2
    low_lanes = iota((RANK, LANES), 1) < 64
    even = jnp.where(core == 0, mine_ref[...], other_ref[...])
    odd = jnp.where(core == 0, other_ref[...], mine_ref[...])
    parts = []
    for p in range(2):
        one, two = even[:, 128 * p : 128 * p + 128], odd[:, 128 * p : 128 * p + 128]
        parts.append(jnp.where(low_lanes, one, pltpu.roll(two, 64, 1)))
        parts.append(jnp.where(low_lanes, pltpu.roll(one, 64, 1), two))
    m = jnp.concatenate(parts, axis=1)
    a = jnp.dot(inv_ref[...], m, precision=HIGH, preferred_element_type=F32)
    for q in range(4):
        pair = a[:, 128 * q : 128 * q + 128]
        scratch[2 * q] = pair
        scratch[2 * q + 1] = pltpu.roll(pair, 64, 1)
    a_ref[...] = scratch[ka]
    gram = folded_gram(a)
    c = c_ref[...]
    highs, lows = [], []
    for k in range(8):
        high, low = split(a * c[:, k : k + 1])
        highs.append(high)
        lows.append(low)
    left = jnp.concatenate([jnp.concatenate(highs, axis=1), jnp.concatenate(lows, axis=1)], axis=0)
    both = jnp.dot(left, t_ref[...].reshape(4096, 512), preferred_element_type=F32)
    out = both[:RANK] + both[RANK:]
    for q in range(4):
        quarters[q] = out[:, 128 * q : 128 * q + 128]
    for n, ref in enumerate((p0_ref, p1_ref, p2_ref, p3_ref)):
        ref[:RANK] = quarters[(ia + n) % 4]
        ref[RANK:] = gram


def sum_kernel(p0_ref, p1_ref, p2_ref, p3_ref, u_ref, gram_ref):
    p = (p0_ref[...] + p1_ref[...]) + (p2_ref[...] + p3_ref[...])
    for n in range(8):
        u_ref[n] = p[:RANK]
    gram_ref[...] = p[RANK:]


def second_solve_kernel(total_i, u_ref, gram_ref, gram_c_ref, ss_ref, scale_ref):
    half = lax.axis_index("ka") % 2
    gram = unfold(gram_ref[...])
    diag = jnp.where(iota(gram.shape, 0) == iota(gram.shape, 1), gram, 0.0)
    scale_col = 1.0 / jnp.sqrt(jnp.sum(diag, axis=1, keepdims=True) / total_i + EPS)
    scale_row = 1.0 / jnp.sqrt(jnp.sum(diag, axis=0, keepdims=True) / total_i + EPS)
    inv = inverse(gram * scale_col * scale_row * gram_c_ref[...])
    scale_ref[...] = jnp.broadcast_to(scale_col, (RANK, LANES))
    m = total(u_ref) * scale_col
    raw = jnp.dot(inv, m, precision=HIGH, preferred_element_type=F32)
    ss = jnp.sum(raw * raw, axis=1, keepdims=True)
    place = iota((RANK, LANES), 0) == iota((RANK, LANES), 1)
    ss_row = jnp.sum(jnp.where(place, ss, 0.0), axis=0, keepdims=True)
    raw = jnp.where(half == 0, raw, pltpu.roll(raw, 64, 1))
    turned_raw = pltpu.roll(raw, 64, 1)
    low_lanes = iota((4, LANES), 1) < 64
    for ia in range(4):
        data = jnp.where(low_lanes, raw[8 * ia : 8 * ia + 4], turned_raw[8 * ia + 4 : 8 * ia + 8])
        tile = jnp.concatenate([data, ss_row], axis=0)
        for ja in range(8):
            start = 5 * (8 * ia + ja)
            ss_ref[start : start + 5] = tile


def finish_kernel(total_j, ss_ref, a_ref, scale_ref, out_a_ref, out_b_ref):
    ia, ja, ka = lax.axis_index("ia"), lax.axis_index("ja"), lax.axis_index("ka")
    place = iota((8, LANES), 1) == iota((8, LANES), 0) + 8 * ia
    ss_row = jnp.sum(ss_ref[pl.ds(4, 32, stride=5), :], axis=0, keepdims=True)
    ss = jnp.sum(jnp.where(place, ss_row, 0.0), axis=1, keepdims=True)
    data = ss_ref[pl.ds(5 * (8 * (ka // 2) + ja), 4), :]
    b = jnp.concatenate([data, pltpu.roll(data, 64, 1)], axis=0) / jnp.sqrt(ss / total_j + EPS)
    out_b_ref[...] = b[:, :64]
    out_a_ref[...] = pltpu.roll(a_ref[...] * scale_ref[...], (32 - 4 * ja) % 32, 0)[:4, :64]


def call(kernel, outs, *args, scratch=(), cost=None, space=VMEM):
    return pl.pallas_call(
        kernel,
        out_shape=[jax.ShapeDtypeStruct(s, F32) for s in outs],
        in_specs=[space] * len(args),
        out_specs=[VMEM] * len(outs),
        scratch_shapes=scratch,
        cost_estimate=cost,
        compiler_params=pltpu.CompilerParams(vmem_limit_bytes=32 * 1024 * 1024),
    )(*args)


def exchange(x, axes, groups=None):
    return lax.all_to_all(x, axes, 0, 0, tiled=True, axis_index_groups=groups)


def other_core(x):
    return lax.ppermute(x, "ja", [(n, n ^ 1) for n in range(8)])


def turned(x, axis, step):
    size = lax.axis_size(axis)
    return lax.ppermute(x, axis, [(n, (n + step) % size) for n in range(size)])


def body(tensor, factor_b, factor_c):
    total_i = tensor.shape[1] * lax.axis_size("ia")
    total_j = tensor.shape[2] * lax.axis_size("ja")
    factor_b, factor_c = (
        pltpu.with_memory_space_constraint(a, pltpu.HBM) for a in (factor_b, factor_c)
    )
    (y,) = call(
        start_kernel,
        [(160, LANES)],
        factor_b,
        factor_c,
        scratch=[
            pltpu.VMEM(factor_b.shape, F32),
            pltpu.VMEM(factor_c.shape, F32),
            pltpu.SemaphoreType.DMA((2,)),
        ],
        cost=LONG,
        space=HBM,
    )
    y = exchange(y.reshape(32, 1, 5 * LANES), ("ia", "ka")).reshape(160, LANES)
    half = (4, 144, LANES)
    send, extra = call(
        lambda *refs: first_kernel(True, *refs), [half, (16, LANES)], y, tensor
    )
    received = other_core(send)
    (keep,) = call(lambda *refs: first_kernel(False, *refs), [half], y, tensor, extra)
    z = [keep[n] + received[n] for n in range(4)]
    z = [z[0]] + [turned(z[n], "ja", 2 * n) for n in range(1, 4)]
    same_core = [[8 * ja + ka for ja in range(core, 8, 2) for ka in range(8)] for core in range(2)]
    u, gram_b, c_all, c_here = call(
        combine_kernel,
        [(32, 16, LANES), (RANK, RANK), (RANK, 64), (RANK, LANES)],
        *z,
        scratch=[pltpu.VMEM((RANK, LANES), F32)],
    )
    v = exchange(u, ("ja", "ka"), same_core)
    (m,) = call(turn_kernel, [(RANK, 256)], v, cost=LONG)
    inv_a, gram_c = call(invert_a_kernel, [(RANK, RANK), (RANK, RANK)], gram_b, c_all)
    *p, a = call(
        second_kernel,
        [(40, LANES)] * 4 + [(RANK, LANES)],
        m,
        other_core(m),
        inv_a,
        tensor,
        c_here,
        scratch=[pltpu.VMEM((8, RANK, LANES), F32), pltpu.VMEM((4, RANK, LANES), F32)],
    )
    p = [p[0]] + [turned(p[n], "ia", n) for n in range(1, 4)]
    u, gram_a = call(sum_kernel, [(8, RANK, LANES), (8, LANES)], *p)
    u = exchange(u, "ka")
    ss, scale_a = call(
        lambda *refs: second_solve_kernel(total_i, *refs),
        [(160, LANES), (RANK, LANES)],
        u,
        gram_a,
        gram_c,
    )
    ss = exchange(ss.reshape(32, 1, 5 * LANES), ("ia", "ja")).reshape(160, LANES)
    out_a, out_b = call(
        lambda *refs: finish_kernel(total_j, *refs), [(4, 64), (8, 64)], ss, a, scale_a
    )
    return out_a, out_b


def solution(mesh):
    return jax.shard_map(
        body,
        mesh=mesh,
        in_specs=(P("ka", "ia", "ja"), P("ia", ("ja", "ka")), P(("ia", "ja"), "ka")),
        out_specs=(P("ja", ("ia", "ka")), P("ia", ("ja", "ka"))),
        check_vma=False,
    )
```

```python
import jax
import jax.numpy as jnp
from jax import lax
from jax.experimental import pallas as pl
from jax.experimental.pallas import tpu as pltpu
from jax.sharding import PartitionSpec as P

EPS = 1e-06
HIGH = lax.Precision.HIGHEST
F32 = jnp.float32
RANK = 32
LANES = 128
NT = (((1,), (1,)), ((), ()))
VMEM = pl.BlockSpec(memory_space=pltpu.VMEM)
HBM = pl.BlockSpec(memory_space=pltpu.HBM)
LONG = pl.CostEstimate(flops=10**10, bytes_accessed=0, transcendentals=0)


def iota(shape, axis):
    return lax.broadcasted_iota(jnp.int32, shape, axis)


def dot_nt(left, right):
    return lax.dot_general(left, right, NT, precision=HIGH, preferred_element_type=F32)


def split(x):
    high = x.astype(jnp.bfloat16)
    return high, (x - high.astype(F32)).astype(jnp.bfloat16)


def fold(x):
    n = x.shape[0] // 4
    group = iota((n, LANES), 1) // 32
    out = x[:n]
    for q in range(1, 4):
        out = jnp.where(group == q, x[n * q : n * q + n], out)
    return out


def unfold(x):
    parts = [x] + [pltpu.roll(x, LANES - 32 * q, 1) for q in range(1, 4)]
    return jnp.concatenate(parts, axis=0)[:, :32]


def total(ref, *index):
    out = ref[(0, *index)]
    for n in range(1, ref.shape[0]):
        out = out + ref[(n, *index)]
    return out


def folded_gram(x):
    gram = dot_nt(x, x)
    return jnp.concatenate([gram[8 * q : 8 * q + 8] for q in range(4)], axis=1)


def inverse(a):
    size = a.shape[0]
    rows, cols = iota(a.shape, 0), iota(a.shape, 1)
    for start in range(0, size, size // 2):
        spread = {p: jnp.broadcast_to(a[:, p : p + 1], a.shape) for p in range(start, start + size // 2)}
        for p in range(start, start + size // 2):
            col = spread.pop(p)
            scale = 1.0 / col[p : p + 1, :]
            row = jnp.where(cols[:1] == p, 1.0, a[p : p + 1, :]) * scale
            a = jnp.where(cols == p, 0.0, a) - col * row
            a = jnp.where(rows == p, row, a)
            for q, other in spread.items():
                there = other[p : p + 1, :] * scale
                spread[q] = jnp.where(rows == p, there, other - col * there)
    return a


def start_kernel(b_hbm, c_hbm, y_ref, b_ref, c_ref, sems):
    copies = [
        pltpu.make_async_copy(b_hbm, b_ref, sems.at[0]),
        pltpu.make_async_copy(c_hbm, c_ref, sems.at[1]),
    ]
    for copy in copies:
        copy.start()
    for copy in copies:
        copy.wait()
    lane = iota((1, LANES), 1)
    c_tiled = jnp.concatenate([c_ref[...]] * 16, axis=1)
    c_row = jnp.where(lane // 8 == 8 + lax.axis_index("ka"), c_tiled, 0.0)
    b_pairs = jnp.concatenate([b_ref[:4], b_ref[4:]], axis=1)
    tile = jnp.concatenate([b_pairs, c_row], axis=0)
    for n in range(32):
        y_ref[5 * n : 5 * n + 5] = tile


def first_kernel(other, y_ref, t_ref, *refs):
    out_ref, extra_ref = refs if other else refs[::-1]
    ja = lax.axis_index("ja")
    low_lanes = iota((4, LANES), 1) < 64
    b_rows = []
    for ia in range(4):
        starts = [5 * (8 * ia + ka) for ka in range(8)]
        parts = [y_ref[start : start + 4] for start in starts]
        pairs = []
        for one, two in zip(parts[::2], parts[1::2]):
            top = jnp.where(low_lanes, one, pltpu.roll(two, 64, 1))
            bottom = jnp.where(low_lanes, pltpu.roll(one, 64, 1), two)
            pairs.append(jnp.concatenate([top, bottom], axis=0))
        b_rows.append(jnp.concatenate(pairs, axis=1))
    b = jnp.concatenate(b_rows, axis=0)
    if other:
        extra_ref[:8] = folded_gram(b)
        row = iota((8, LANES), 0)
        c_rows = jnp.zeros((8, LANES), F32)
        for ia in range(4):
            starts = [5 * (8 * ia + ka) + 4 for ka in range(8)]
            c_row = sum(y_ref[start : start + 1] for start in starts)
            c_rows = jnp.where(row == 4 * (ja % 2) + ia, c_row, c_rows)
        extra_ref[8:] = c_rows
    extra = extra_ref[...]
    high, low = split(b)

    left = jnp.concatenate([high, low], axis=0)
    core = 1 - ja % 2 if other else ja % 2
    starts = [pl.multiple_of(64 * (2 * ((ja // 2 + n) % 4) + core), 64) for n in range(4)]
    low_lanes = iota((RANK, LANES), 1) < 64
    right = jnp.concatenate(
        [t_ref[k, pl.ds(start, 64), :] for k in range(8) for start in starts], axis=0
    )
    both = lax.dot_general(left, right, NT, preferred_element_type=F32)
    both = both[:RANK] + both[RANK:]
    for pair in range(4):
        products = [both[:, 512 * pair : 512 * pair + 256], both[:, 512 * pair + 256 : 512 * pair + 512]]
        rows = slice(32 * pair, 32 * pair + 32)
        for v in range(2):
            one, two = (x[:, 128 * v : 128 * v + 128] for x in products)
            out_ref[2 * v, rows, :] = jnp.where(low_lanes, one, pltpu.roll(two, 64, 1))
            out_ref[2 * v + 1, rows, :] = jnp.where(low_lanes, pltpu.roll(one, 64, 1), two)
    for n in range(4):
        out_ref[n, 128:144, :] = extra


def combine_kernel(z0_ref, z1_ref, z2_ref, z3_ref, u_ref, gram_ref, c_all_ref, c_ref, scratch):
    ka, y = lax.axis_index("ka"), lax.axis_index("ja") // 2
    for n, ref in enumerate((z0_ref, z1_ref, z2_ref, z3_ref)):
        for core in range(2):
            place = pl.ds(2 * ((y + 4 - n) % 4) + core, 4, stride=8)
            scratch[place, :] = ref[136 + 4 * core : 140 + 4 * core]
    extra = scratch[...]
    z = (z0_ref[...] + z1_ref[...]) + (z2_ref[...] + z3_ref[...])
    gram_ref[...] = unfold(z[128:136])
    c_all_ref[...] = pltpu.roll(extra, 64, 1)[:, :64]
    c_here = pltpu.roll(extra, 64 - 8 * ka, 1)
    c_ref[...] = c_here
    low_lanes = iota((RANK, LANES), 1) < 64
    m = None
    for pair in range(4):
        first, second = c_here[:, 2 * pair : 2 * pair + 1], c_here[:, 2 * pair + 1 : 2 * pair + 2]
        term = z[32 * pair : 32 * pair + 32] * jnp.where(low_lanes, first, second)
        m = term if m is None else m + term
    m = m + pltpu.roll(m, 64, 1)
    u = jnp.where(low_lanes[:16], m[:16], m[16:])
    for n in range(32):
        u_ref[n] = u


def invert_a_kernel(gram_b_ref, c_all_ref, inv_ref, gram_c_ref):
    gram_c = dot_nt(c_all_ref[...], c_all_ref[...])
    gram_c_ref[...] = gram_c
    inv_ref[...] = inverse(gram_b_ref[...] * gram_c)


def turn_kernel(v_ref, m_ref):
    low_lanes = iota((16, LANES), 1) < 64
    parts = []
    for y in range(4):
        part = v_ref[8 * y]
        for ka in range(1, 8):
            part = part + v_ref[8 * y + ka]
        parts.append(part)
    for p in range(2):
        one, two = parts[2 * p], parts[2 * p + 1]
        m_ref[:16, 128 * p : 128 * p + 128] = jnp.where(low_lanes, one, pltpu.roll(two, 64, 1))
        m_ref[16:, 128 * p : 128 * p + 128] = jnp.where(low_lanes, pltpu.roll(one, 64, 1), two)


def second_kernel(
    mine_ref, other_ref, inv_ref, t_ref, c_ref, p0_ref, p1_ref, p2_ref, p3_ref, a_ref, scratch, quarters
):
    ia, ka, core = lax.axis_index("ia"), lax.axis_index("ka"), lax.axis_index("ja") % 2
    low_lanes = iota((RANK, LANES), 1) < 64
    even = jnp.where(core == 0, mine_ref[...], other_ref[...])
    odd = jnp.where(core == 0, other_ref[...], mine_ref[...])
    parts = []
    for p in range(2):
        one, two = even[:, 128 * p : 128 * p + 128], odd[:, 128 * p : 128 * p + 128]
        parts.append(jnp.where(low_lanes, one, pltpu.roll(two, 64, 1)))
        parts.append(jnp.where(low_lanes, pltpu.roll(one, 64, 1), two))
    m = jnp.concatenate(parts, axis=1)
    a = jnp.dot(inv_ref[...], m, precision=HIGH, preferred_element_type=F32)
    for q in range(4):
        pair = a[:, 128 * q : 128 * q + 128]
        scratch[2 * q] = pair
        scratch[2 * q + 1] = pltpu.roll(pair, 64, 1)
    a_ref[...] = scratch[ka]
    gram = folded_gram(a)
    c = c_ref[...]
    highs, lows = [], []
    for k in range(8):
        high, low = split(a * c[:, k : k + 1])
        highs.append(high)
        lows.append(low)
    left = jnp.concatenate([jnp.concatenate(highs, axis=1), jnp.concatenate(lows, axis=1)], axis=0)
    both = jnp.dot(left, t_ref[...].reshape(4096, 512), preferred_element_type=F32)
    out = both[:RANK] + both[RANK:]
    for q in range(4):
        quarters[q] = out[:, 128 * q : 128 * q + 128]
    for n, ref in enumerate((p0_ref, p1_ref, p2_ref, p3_ref)):
        ref[:RANK] = quarters[(ia + n) % 4]
        ref[RANK:] = gram


def sum_kernel(p0_ref, p1_ref, p2_ref, p3_ref, u_ref, gram_ref):
    p = (p0_ref[...] + p1_ref[...]) + (p2_ref[...] + p3_ref[...])
    for n in range(8):
        u_ref[n] = p[:RANK]
    gram_ref[...] = p[RANK:]


def second_solve_kernel(total_i, u_ref, gram_ref, gram_c_ref, ss_ref, scale_ref):
    half = lax.axis_index("ka") % 2
    gram = unfold(gram_ref[...])
    diag = jnp.where(iota(gram.shape, 0) == iota(gram.shape, 1), gram, 0.0)
    scale_col = lax.rsqrt(jnp.sum(diag, axis=1, keepdims=True) / total_i + EPS)
    scale_row = lax.rsqrt(jnp.sum(diag, axis=0, keepdims=True) / total_i + EPS)
    inv = inverse(gram * scale_col * scale_row * gram_c_ref[...])
    scale_ref[...] = jnp.broadcast_to(scale_col, (RANK, LANES))
    m = total(u_ref) * scale_col
    raw = jnp.dot(inv, m, precision=HIGH, preferred_element_type=F32)
    ss = jnp.sum(raw * raw, axis=1, keepdims=True)
    place = iota((RANK, LANES), 0) == iota((RANK, LANES), 1)
    ss_row = jnp.sum(jnp.where(place, ss, 0.0), axis=0, keepdims=True)
    raw = jnp.where(half == 0, raw, pltpu.roll(raw, 64, 1))
    turned_raw = pltpu.roll(raw, 64, 1)
    low_lanes = iota((4, LANES), 1) < 64
    for ia in range(4):
        data = jnp.where(low_lanes, raw[8 * ia : 8 * ia + 4], turned_raw[8 * ia + 4 : 8 * ia + 8])
        tile = jnp.concatenate([data, ss_row], axis=0)
        for ja in range(8):
            start = 5 * (8 * ia + ja)
            ss_ref[start : start + 5] = tile


def finish_kernel(total_j, ss_ref, a_ref, scale_ref, out_a_ref, out_b_ref):
    ia, ja, ka = lax.axis_index("ia"), lax.axis_index("ja"), lax.axis_index("ka")
    place = iota((8, LANES), 1) == iota((8, LANES), 0) + 8 * ia
    ss_row = jnp.sum(ss_ref[pl.ds(4, 32, stride=5), :], axis=0, keepdims=True)
    ss = jnp.sum(jnp.where(place, ss_row, 0.0), axis=1, keepdims=True)
    data = ss_ref[pl.ds(5 * (8 * (ka // 2) + ja), 4), :]
    b = jnp.concatenate([data, pltpu.roll(data, 64, 1)], axis=0) / jnp.sqrt(ss / total_j + EPS)
    out_b_ref[...] = b[:, :64]
    out_a_ref[...] = pltpu.roll(a_ref[...] * scale_ref[...], (32 - 4 * ja) % 32, 0)[:4, :64]


def call(kernel, outs, *args, scratch=(), cost=None, space=VMEM):
    return pl.pallas_call(
        kernel,
        out_shape=[jax.ShapeDtypeStruct(s, F32) for s in outs],
        in_specs=[space] * len(args),
        out_specs=[VMEM] * len(outs),
        scratch_shapes=scratch,
        cost_estimate=cost,
        compiler_params=pltpu.CompilerParams(vmem_limit_bytes=32 * 1024 * 1024),
    )(*args)


def exchange(x, axes, groups=None):
    return lax.all_to_all(x, axes, 0, 0, tiled=True, axis_index_groups=groups)


def other_core(x):
    return lax.ppermute(x, "ja", [(n, n ^ 1) for n in range(8)])


def turned(x, axis, step):
    size = lax.axis_size(axis)
    return lax.ppermute(x, axis, [(n, (n + step) % size) for n in range(size)])


def body(tensor, factor_b, factor_c):
    total_i = tensor.shape[1] * lax.axis_size("ia")
    total_j = tensor.shape[2] * lax.axis_size("ja")
    factor_b, factor_c = (
        pltpu.with_memory_space_constraint(a, pltpu.HBM) for a in (factor_b, factor_c)
    )
    (y,) = call(
        start_kernel,
        [(160, LANES)],
        factor_b,
        factor_c,
        scratch=[
            pltpu.VMEM(factor_b.shape, F32),
            pltpu.VMEM(factor_c.shape, F32),
            pltpu.SemaphoreType.DMA((2,)),
        ],
        cost=LONG,
        space=HBM,
    )
    y = exchange(y.reshape(32, 1, 5 * LANES), ("ia", "ka")).reshape(160, LANES)
    half = (4, 144, LANES)
    send, extra = call(
        lambda *refs: first_kernel(True, *refs), [half, (16, LANES)], y, tensor
    )
    received = other_core(send)
    (keep,) = call(lambda *refs: first_kernel(False, *refs), [half], y, tensor, extra)
    z = [keep[n] + received[n] for n in range(4)]
    z = [z[0]] + [turned(z[n], "ja", 2 * n) for n in range(1, 4)]
    same_core = [[8 * ja + ka for ja in range(core, 8, 2) for ka in range(8)] for core in range(2)]
    u, gram_b, c_all, c_here = call(
        combine_kernel,
        [(32, 16, LANES), (RANK, RANK), (RANK, 64), (RANK, LANES)],
        *z,
        scratch=[pltpu.VMEM((RANK, LANES), F32)],
    )
    v = exchange(u, ("ja", "ka"), same_core)
    (m,) = call(turn_kernel, [(RANK, 256)], v, cost=LONG)
    inv_a, gram_c = call(invert_a_kernel, [(RANK, RANK), (RANK, RANK)], gram_b, c_all)
    *p, a = call(
        second_kernel,
        [(40, LANES)] * 4 + [(RANK, LANES)],
        m,
        other_core(m),
        inv_a,
        tensor,
        c_here,
        scratch=[pltpu.VMEM((8, RANK, LANES), F32), pltpu.VMEM((4, RANK, LANES), F32)],
    )
    p = [p[0]] + [turned(p[n], "ia", n) for n in range(1, 4)]
    u, gram_a = call(sum_kernel, [(8, RANK, LANES), (8, LANES)], *p)
    u = exchange(u, "ka")
    ss, scale_a = call(
        lambda *refs: second_solve_kernel(total_i, *refs),
        [(160, LANES), (RANK, LANES)],
        u,
        gram_a,
        gram_c,
    )
    ss = exchange(ss.reshape(32, 1, 5 * LANES), ("ia", "ja")).reshape(160, LANES)
    out_a, out_b = call(
        lambda *refs: finish_kernel(total_j, *refs), [(4, 64), (8, 64)], ss, a, scale_a
    )
    return out_a, out_b


def solution(mesh):
    return jax.shard_map(
        body,
        mesh=mesh,
        in_specs=(P("ka", "ia", "ja"), P("ia", ("ja", "ka")), P(("ia", "ja"), "ka")),
        out_specs=(P("ja", ("ia", "ka")), P("ia", ("ja", "ka"))),
        check_vma=False,
    )
```

```python
import jax
import jax.numpy as jnp
from jax import lax
from jax.experimental import pallas as pl
from jax.experimental.pallas import tpu as pltpu
from jax.sharding import PartitionSpec as P

EPS = 1e-06
HIGH = lax.Precision.HIGHEST
F32 = jnp.float32
RANK = 32
LANES = 128
NT = (((1,), (1,)), ((), ()))
VMEM = pl.BlockSpec(memory_space=pltpu.VMEM)
HBM = pl.BlockSpec(memory_space=pltpu.HBM)
LONG = pl.CostEstimate(flops=10**10, bytes_accessed=0, transcendentals=0)


def iota(shape, axis):
    return lax.broadcasted_iota(jnp.int32, shape, axis)


def dot_nt(left, right):
    return lax.dot_general(left, right, NT, precision=HIGH, preferred_element_type=F32)


def split(x):
    high = x.astype(jnp.bfloat16)
    return high, (x - high.astype(F32)).astype(jnp.bfloat16)


def fold(x):
    n = x.shape[0] // 4
    group = iota((n, LANES), 1) // 32
    out = x[:n]
    for q in range(1, 4):
        out = jnp.where(group == q, x[n * q : n * q + n], out)
    return out


def unfold(x):
    parts = [x] + [pltpu.roll(x, LANES - 32 * q, 1) for q in range(1, 4)]
    return jnp.concatenate(parts, axis=0)[:, :32]


def total(ref, *index):
    out = ref[(0, *index)]
    for n in range(1, ref.shape[0]):
        out = out + ref[(n, *index)]
    return out


def folded_gram(x):
    gram = dot_nt(x, x)
    return jnp.concatenate([gram[8 * q : 8 * q + 8] for q in range(4)], axis=1)


def inverse(a):
    size = a.shape[0]
    rows, cols = iota(a.shape, 0), iota(a.shape, 1)
    for start in range(0, size, size // 2):
        spread = {p: jnp.broadcast_to(a[:, p : p + 1], a.shape) for p in range(start, start + size // 2)}
        for p in range(start, start + size // 2):
            col = spread.pop(p)
            scale = 1.0 / col[p : p + 1, :]
            row = jnp.where(cols[:1] == p, 1.0, a[p : p + 1, :]) * scale
            a = jnp.where(cols == p, 0.0, a) - col * row
            a = jnp.where(rows == p, row, a)
            for q, other in spread.items():
                there = other[p : p + 1, :] * scale
                spread[q] = jnp.where(rows == p, there, other - col * there)
    return a


def start_kernel(b_hbm, c_hbm, y_ref, b_ref, c_ref, sems):
    copies = [
        pltpu.make_async_copy(b_hbm, b_ref, sems.at[0]),
        pltpu.make_async_copy(c_hbm, c_ref, sems.at[1]),
    ]
    for copy in copies:
        copy.start()
    for copy in copies:
        copy.wait()
    lane = iota((1, LANES), 1)
    c_tiled = jnp.concatenate([c_ref[...]] * 16, axis=1)
    c_row = jnp.where(lane // 8 == 8 + lax.axis_index("ka"), c_tiled, 0.0)
    b_pairs = jnp.concatenate([b_ref[:4], b_ref[4:]], axis=1)
    tile = jnp.concatenate([b_pairs, c_row], axis=0)
    for n in range(32):
        y_ref[5 * n : 5 * n + 5] = tile


def first_kernel(other, y_ref, t_ref, *refs):
    out_ref, extra_ref = refs if other else refs[::-1]
    ja = lax.axis_index("ja")
    low_lanes = iota((4, LANES), 1) < 64
    b_rows = []
    for ia in range(4):
        starts = [5 * (8 * ia + ka) for ka in range(8)]
        parts = [y_ref[start : start + 4] for start in starts]
        pairs = []
        for one, two in zip(parts[::2], parts[1::2]):
            top = jnp.where(low_lanes, one, pltpu.roll(two, 64, 1))
            bottom = jnp.where(low_lanes, pltpu.roll(one, 64, 1), two)
            pairs.append(jnp.concatenate([top, bottom], axis=0))
        b_rows.append(jnp.concatenate(pairs, axis=1))
    b = jnp.concatenate(b_rows, axis=0)
    if other:
        extra_ref[:8] = folded_gram(b)
        row = iota((8, LANES), 0)
        c_rows = jnp.zeros((8, LANES), F32)
        c_parts = y_ref[pl.ds(4, 32, stride=5), :]
        for ia in range(4):
            c_row = jnp.sum(c_parts[8 * ia : 8 * ia + 8], axis=0, keepdims=True)
            c_rows = jnp.where(row == 4 * (ja % 2) + ia, c_row, c_rows)
        extra_ref[8:] = c_rows
    extra = extra_ref[...]
    high, low = split(b)

    def placed(part, q):
        zeros = jnp.zeros((RANK, 512), jnp.bfloat16)
        return [part if n == q else zeros for n in range(4)]

    weights = jnp.concatenate(
        [jnp.concatenate(placed(high, q) + placed(low, q), axis=0) for q in range(4)], axis=1
    )
    core = 1 - ja % 2 if other else ja % 2
    starts = [pl.multiple_of(64 * (2 * ((ja // 2 + n) % 4) + core), 64) for n in range(4)]
    for h in range(2):
        left = jnp.concatenate(
            [
                jnp.concatenate([t_ref[4 * h + q, pl.ds(start, 64), :] for start in starts], axis=0)
                for q in range(4)
            ],
            axis=1,
        )
        both = lax.dot_general(left, weights, NT, preferred_element_type=F32)
        y = both[:, :LANES] + both[:, LANES:]
        for n in range(4):
            out_ref[n, 64 * h : 64 * h + 64, :] = y[64 * n : 64 * n + 64]
    for n in range(4):
        out_ref[n, 128:144, :] = extra


def combine_kernel(z0_ref, z1_ref, z2_ref, z3_ref, u_ref, gram_ref, c_all_ref, c_ref, scratch):
    ka, y = lax.axis_index("ka"), lax.axis_index("ja") // 2
    for n, ref in enumerate((z0_ref, z1_ref, z2_ref, z3_ref)):
        for core in range(2):
            place = pl.ds(2 * ((y + 4 - n) % 4) + core, 4, stride=8)
            scratch[place, :] = ref[136 + 4 * core : 140 + 4 * core]
    extra = scratch[...]
    z = (z0_ref[...] + z1_ref[...]) + (z2_ref[...] + z3_ref[...])
    gram_ref[...] = unfold(z[128:136])
    c_all_ref[...] = pltpu.roll(extra, 64, 1)[:, :64]
    c_here = pltpu.roll(extra, 64 - 8 * ka, 1)
    c_ref[...] = c_here
    c_t = c_here.T[:8]
    c_tiled = jnp.concatenate([c_t] * 4, axis=1)
    which = iota((8, LANES), 0) - iota((8, LANES), 1) // 32
    acc = None
    for h in range(2):
        weight = jnp.sum(jnp.where(which == 4 * h, c_tiled, 0.0), axis=0, keepdims=True)
        term = z[64 * h : 64 * h + 64] * weight
        acc = term if acc is None else acc + term
    acc = acc + pltpu.roll(acc, 64, 1)
    acc = acc + pltpu.roll(acc, 32, 1)
    u = fold(acc)
    for n in range(32):
        u_ref[n] = u


def invert_a_kernel(gram_b_ref, c_all_ref, inv_ref, gram_c_ref):
    gram_c = dot_nt(c_all_ref[...], c_all_ref[...])
    gram_c_ref[...] = gram_c
    inv_ref[...] = inverse(gram_b_ref[...] * gram_c)


def turn_kernel(v_ref, m_ref):
    parts = []
    for y in range(4):
        part = v_ref[8 * y]
        for ka in range(1, 8):
            part = part + v_ref[8 * y + ka]
        parts.append(unfold(part))
    m_ref[...] = jnp.concatenate(parts, axis=0).T


def second_kernel(
    mine_ref, other_ref, inv_ref, t_ref, c_ref, p0_ref, p1_ref, p2_ref, p3_ref, a_ref, scratch, quarters
):
    ia, ka, core = lax.axis_index("ia"), lax.axis_index("ka"), lax.axis_index("ja") % 2
    low_lanes = iota((RANK, LANES), 1) < 64
    even = jnp.where(core == 0, mine_ref[...], other_ref[...])
    odd = jnp.where(core == 0, other_ref[...], mine_ref[...])
    parts = []
    for p in range(2):
        one, two = even[:, 128 * p : 128 * p + 128], odd[:, 128 * p : 128 * p + 128]
        parts.append(jnp.where(low_lanes, one, pltpu.roll(two, 64, 1)))
        parts.append(jnp.where(low_lanes, pltpu.roll(one, 64, 1), two))
    m = jnp.concatenate(parts, axis=1)
    a = jnp.dot(inv_ref[...], m, precision=HIGH, preferred_element_type=F32)
    for q in range(4):
        pair = a[:, 128 * q : 128 * q + 128]
        scratch[2 * q] = pair
        scratch[2 * q + 1] = pltpu.roll(pair, 64, 1)
    a_ref[...] = scratch[ka]
    gram = folded_gram(a)
    c = c_ref[...]
    highs, lows = [], []
    for k in range(8):
        high, low = split(a * c[:, k : k + 1])
        highs.append(high)
        lows.append(low)
    left = jnp.concatenate([jnp.concatenate(highs, axis=1), jnp.concatenate(lows, axis=1)], axis=0)
    both = jnp.dot(left, t_ref[...].reshape(4096, 512), preferred_element_type=F32)
    out = both[:RANK] + both[RANK:]
    for q in range(4):
        quarters[q] = out[:, 128 * q : 128 * q + 128]
    for n, ref in enumerate((p0_ref, p1_ref, p2_ref, p3_ref)):
        ref[:RANK] = quarters[(ia + n) % 4]
        ref[RANK:] = gram


def sum_kernel(p0_ref, p1_ref, p2_ref, p3_ref, u_ref, gram_ref):
    p = (p0_ref[...] + p1_ref[...]) + (p2_ref[...] + p3_ref[...])
    for n in range(8):
        u_ref[n] = p[:RANK]
    gram_ref[...] = p[RANK:]


def second_solve_kernel(total_i, u_ref, gram_ref, gram_c_ref, ss_ref, scale_ref):
    half = lax.axis_index("ka") % 2
    gram = unfold(gram_ref[...])
    diag = jnp.where(iota(gram.shape, 0) == iota(gram.shape, 1), gram, 0.0)
    scale_col = lax.rsqrt(jnp.sum(diag, axis=1, keepdims=True) / total_i + EPS)
    scale_row = lax.rsqrt(jnp.sum(diag, axis=0, keepdims=True) / total_i + EPS)
    inv = inverse(gram * scale_col * scale_row * gram_c_ref[...])
    scale_ref[...] = jnp.broadcast_to(scale_col, (RANK, LANES))
    m = total(u_ref) * scale_col
    raw = jnp.dot(inv, m, precision=HIGH, preferred_element_type=F32)
    ss = jnp.sum(raw * raw, axis=1, keepdims=True)
    place = iota((RANK, LANES), 0) == iota((RANK, LANES), 1)
    ss_row = jnp.sum(jnp.where(place, ss, 0.0), axis=0, keepdims=True)
    raw = jnp.where(half == 0, raw, pltpu.roll(raw, 64, 1))
    turned_raw = pltpu.roll(raw, 64, 1)
    low_lanes = iota((4, LANES), 1) < 64
    for ia in range(4):
        data = jnp.where(low_lanes, raw[8 * ia : 8 * ia + 4], turned_raw[8 * ia + 4 : 8 * ia + 8])
        tile = jnp.concatenate([data, ss_row], axis=0)
        for ja in range(8):
            start = 5 * (8 * ia + ja)
            ss_ref[start : start + 5] = tile


def finish_kernel(total_j, ss_ref, a_ref, scale_ref, out_a_ref, out_b_ref):
    ia, ja, ka = lax.axis_index("ia"), lax.axis_index("ja"), lax.axis_index("ka")
    place = iota((8, LANES), 1) == iota((8, LANES), 0) + 8 * ia
    ss_row = jnp.sum(ss_ref[pl.ds(4, 32, stride=5), :], axis=0, keepdims=True)
    ss = jnp.sum(jnp.where(place, ss_row, 0.0), axis=1, keepdims=True)
    data = ss_ref[pl.ds(5 * (8 * (ka // 2) + ja), 4), :]
    b = jnp.concatenate([data, pltpu.roll(data, 64, 1)], axis=0) / jnp.sqrt(ss / total_j + EPS)
    out_b_ref[...] = b[:, :64]
    out_a_ref[...] = pltpu.roll(a_ref[...] * scale_ref[...], (32 - 4 * ja) % 32, 0)[:4, :64]


def call(kernel, outs, *args, scratch=(), cost=None, space=VMEM):
    return pl.pallas_call(
        kernel,
        out_shape=[jax.ShapeDtypeStruct(s, F32) for s in outs],
        in_specs=[space] * len(args),
        out_specs=[VMEM] * len(outs),
        scratch_shapes=scratch,
        cost_estimate=cost,
        compiler_params=pltpu.CompilerParams(vmem_limit_bytes=32 * 1024 * 1024),
    )(*args)


def exchange(x, axes, groups=None):
    return lax.all_to_all(x, axes, 0, 0, tiled=True, axis_index_groups=groups)


def other_core(x):
    return lax.ppermute(x, "ja", [(n, n ^ 1) for n in range(8)])


def turned(x, axis, step):
    size = lax.axis_size(axis)
    return lax.ppermute(x, axis, [(n, (n + step) % size) for n in range(size)])


def body(tensor, factor_b, factor_c):
    total_i = tensor.shape[1] * lax.axis_size("ia")
    total_j = tensor.shape[2] * lax.axis_size("ja")
    factor_b, factor_c = (
        pltpu.with_memory_space_constraint(a, pltpu.HBM) for a in (factor_b, factor_c)
    )
    (y,) = call(
        start_kernel,
        [(160, LANES)],
        factor_b,
        factor_c,
        scratch=[
            pltpu.VMEM(factor_b.shape, F32),
            pltpu.VMEM(factor_c.shape, F32),
            pltpu.SemaphoreType.DMA((2,)),
        ],
        cost=LONG,
        space=HBM,
    )
    y = exchange(y.reshape(32, 1, 5 * LANES), ("ia", "ka")).reshape(160, LANES)
    half = (4, 144, LANES)
    send, extra = call(
        lambda *refs: first_kernel(True, *refs), [half, (16, LANES)], y, tensor
    )
    received = other_core(send)
    (keep,) = call(lambda *refs: first_kernel(False, *refs), [half], y, tensor, extra)
    z = [keep[n] + received[n] for n in range(4)]
    z = [z[0]] + [turned(z[n], "ja", 2 * n) for n in range(1, 4)]
    same_core = [[8 * ja + ka for ja in range(core, 8, 2) for ka in range(8)] for core in range(2)]
    u, gram_b, c_all, c_here = call(
        combine_kernel,
        [(32, 16, LANES), (RANK, RANK), (RANK, 64), (RANK, LANES)],
        *z,
        scratch=[pltpu.VMEM((RANK, LANES), F32)],
    )
    v = exchange(u, ("ja", "ka"), same_core)
    (m,) = call(turn_kernel, [(RANK, 256)], v, cost=LONG)
    inv_a, gram_c = call(invert_a_kernel, [(RANK, RANK), (RANK, RANK)], gram_b, c_all)
    *p, a = call(
        second_kernel,
        [(40, LANES)] * 4 + [(RANK, LANES)],
        m,
        other_core(m),
        inv_a,
        tensor,
        c_here,
        scratch=[pltpu.VMEM((8, RANK, LANES), F32), pltpu.VMEM((4, RANK, LANES), F32)],
    )
    p = [p[0]] + [turned(p[n], "ia", n) for n in range(1, 4)]
    u, gram_a = call(sum_kernel, [(8, RANK, LANES), (8, LANES)], *p)
    u = exchange(u, "ka")
    ss, scale_a = call(
        lambda *refs: second_solve_kernel(total_i, *refs),
        [(160, LANES), (RANK, LANES)],
        u,
        gram_a,
        gram_c,
    )
    ss = exchange(ss.reshape(32, 1, 5 * LANES), ("ia", "ja")).reshape(160, LANES)
    out_a, out_b = call(
        lambda *refs: finish_kernel(total_j, *refs), [(4, 64), (8, 64)], ss, a, scale_a
    )
    return out_a, out_b


def solution(mesh):
    return jax.shard_map(
        body,
        mesh=mesh,
        in_specs=(P("ka", "ia", "ja"), P("ia", ("ja", "ka")), P(("ia", "ja"), "ka")),
        out_specs=(P("ja", ("ia", "ka")), P("ia", ("ja", "ka"))),
        check_vma=False,
    )
```

```python
import jax
import jax.numpy as jnp
from jax import lax
from jax.experimental import pallas as pl
from jax.experimental.pallas import tpu as pltpu
from jax.sharding import PartitionSpec as P

EPS = 1e-06
HIGH = lax.Precision.HIGHEST
F32 = jnp.float32
RANK = 32
LANES = 128
NT = (((1,), (1,)), ((), ()))
VMEM = pl.BlockSpec(memory_space=pltpu.VMEM)
HBM = pl.BlockSpec(memory_space=pltpu.HBM)
LONG = pl.CostEstimate(flops=10**10, bytes_accessed=0, transcendentals=0)


def iota(shape, axis):
    return lax.broadcasted_iota(jnp.int32, shape, axis)


def dot_nt(left, right):
    return lax.dot_general(left, right, NT, precision=HIGH, preferred_element_type=F32)


def split(x):
    high = x.astype(jnp.bfloat16)
    return high, (x - high.astype(F32)).astype(jnp.bfloat16)


def fold(x):
    n = x.shape[0] // 4
    group = iota((n, LANES), 1) // 32
    out = x[:n]
    for q in range(1, 4):
        out = jnp.where(group == q, x[n * q : n * q + n], out)
    return out


def unfold(x):
    parts = [x] + [pltpu.roll(x, LANES - 32 * q, 1) for q in range(1, 4)]
    return jnp.concatenate(parts, axis=0)[:, :32]


def total(ref, *index):
    out = ref[(0, *index)]
    for n in range(1, ref.shape[0]):
        out = out + ref[(n, *index)]
    return out


def folded_gram(x):
    gram = dot_nt(x, x)
    return jnp.concatenate([gram[8 * q : 8 * q + 8] for q in range(4)], axis=1)


def inverse(a):
    size = a.shape[0]
    rows, cols = iota(a.shape, 0), iota(a.shape, 1)
    for start in range(0, size, size // 2):
        spread = {p: jnp.broadcast_to(a[:, p : p + 1], a.shape) for p in range(start, start + size // 2)}
        for p in range(start, start + size // 2):
            col = spread.pop(p)
            scale = 1.0 / col[p : p + 1, :]
            row = jnp.where(cols[:1] == p, 1.0, a[p : p + 1, :]) * scale
            a = jnp.where(cols == p, 0.0, a) - col * row
            a = jnp.where(rows == p, row, a)
            for q, other in spread.items():
                there = other[p : p + 1, :] * scale
                spread[q] = jnp.where(rows == p, there, other - col * there)
    return a


def start_kernel(b_hbm, c_hbm, y_ref, b_ref, c_ref, sems):
    copies = [
        pltpu.make_async_copy(b_hbm, b_ref, sems.at[0]),
        pltpu.make_async_copy(c_hbm, c_ref, sems.at[1]),
    ]
    for copy in copies:
        copy.start()
    for copy in copies:
        copy.wait()
    lane = iota((1, LANES), 1)
    c_tiled = jnp.concatenate([c_ref[...]] * 16, axis=1)
    c_row = jnp.where(lane // 8 == 8 + lax.axis_index("ka"), c_tiled, 0.0)
    b_pairs = jnp.concatenate([b_ref[:4], b_ref[4:]], axis=1)
    tile = jnp.concatenate([b_pairs, c_row], axis=0)
    block = jnp.concatenate([tile] * 8, axis=0)
    for n in range(4):
        y_ref[40 * n : 40 * n + 40] = block


def first_kernel(other, y_ref, t_ref, *refs):
    out_ref, extra_ref = refs if other else refs[::-1]
    ja = lax.axis_index("ja")
    low_lanes = iota((4, LANES), 1) < 64
    b_rows = []
    for ia in range(4):
        starts = [5 * (8 * ia + ka) for ka in range(8)]
        parts = [y_ref[start : start + 4] for start in starts]
        pairs = []
        for one, two in zip(parts[::2], parts[1::2]):
            top = jnp.where(low_lanes, one, pltpu.roll(two, 64, 1))
            bottom = jnp.where(low_lanes, pltpu.roll(one, 64, 1), two)
            pairs.append(jnp.concatenate([top, bottom], axis=0))
        b_rows.append(jnp.concatenate(pairs, axis=1))
    b = jnp.concatenate(b_rows, axis=0)
    if other:
        extra_ref[:8] = folded_gram(b)
        row = iota((8, LANES), 0)
        c_rows = jnp.zeros((8, LANES), F32)
        c_parts = y_ref[pl.ds(4, 32, stride=5), :]
        for ia in range(4):
            c_row = jnp.sum(c_parts[8 * ia : 8 * ia + 8], axis=0, keepdims=True)
            c_rows = jnp.where(row == 4 * (ja % 2) + ia, c_row, c_rows)
        extra_ref[8:] = c_rows
    extra = extra_ref[...]
    high, low = split(b)

    def placed(part, q):
        zeros = jnp.zeros((RANK, 512), jnp.bfloat16)
        return [part if n == q else zeros for n in range(4)]

    weights = jnp.concatenate(
        [jnp.concatenate(placed(high, q) + placed(low, q), axis=0) for q in range(4)], axis=1
    )
    core = 1 - ja % 2 if other else ja % 2
    starts = [pl.multiple_of(64 * (2 * ((ja // 2 + n) % 4) + core), 64) for n in range(4)]
    for h in range(2):
        left = jnp.concatenate(
            [
                jnp.concatenate([t_ref[4 * h + q, pl.ds(start, 64), :] for start in starts], axis=0)
                for q in range(4)
            ],
            axis=1,
        )
        both = lax.dot_general(left, weights, NT, preferred_element_type=F32)
        y = both[:, :LANES] + both[:, LANES:]
        for n in range(4):
            out_ref[n, 64 * h : 64 * h + 64, :] = y[64 * n : 64 * n + 64]
    for n in range(4):
        out_ref[n, 128:144, :] = extra


def combine_kernel(z0_ref, z1_ref, z2_ref, z3_ref, u_ref, gram_ref, c_all_ref, c_ref, scratch):
    ka, y = lax.axis_index("ka"), lax.axis_index("ja") // 2
    for n, ref in enumerate((z0_ref, z1_ref, z2_ref, z3_ref)):
        for core in range(2):
            place = pl.ds(2 * ((y + 4 - n) % 4) + core, 4, stride=8)
            scratch[place, :] = ref[136 + 4 * core : 140 + 4 * core]
    extra = scratch[...]
    z = (z0_ref[...] + z1_ref[...]) + (z2_ref[...] + z3_ref[...])
    gram_ref[...] = unfold(z[128:136])
    c_all_ref[...] = pltpu.roll(extra, 64, 1)[:, :64]
    c_here = pltpu.roll(extra, 64 - 8 * ka, 1)
    c_ref[...] = c_here
    c_t = c_here.T[:8]
    c_tiled = jnp.concatenate([c_t] * 4, axis=1)
    which = iota((8, LANES), 0) - iota((8, LANES), 1) // 32
    acc = None
    for h in range(2):
        weight = jnp.sum(jnp.where(which == 4 * h, c_tiled, 0.0), axis=0, keepdims=True)
        term = z[64 * h : 64 * h + 64] * weight
        acc = term if acc is None else acc + term
    acc = acc + pltpu.roll(acc, 64, 1)
    acc = acc + pltpu.roll(acc, 32, 1)
    u = fold(acc)
    for n in range(32):
        u_ref[n] = u


def invert_a_kernel(gram_b_ref, c_all_ref, inv_ref, gram_c_ref):
    gram_c = dot_nt(c_all_ref[...], c_all_ref[...])
    gram_c_ref[...] = gram_c
    inv_ref[...] = inverse(gram_b_ref[...] * gram_c)


def turn_kernel(v_ref, m_ref):
    parts = []
    for y in range(4):
        part = v_ref[8 * y]
        for ka in range(1, 8):
            part = part + v_ref[8 * y + ka]
        parts.append(unfold(part))
    m_ref[...] = jnp.concatenate(parts, axis=0).T


def second_kernel(
    mine_ref, other_ref, inv_ref, t_ref, c_ref, p0_ref, p1_ref, p2_ref, p3_ref, a_ref, scratch, quarters
):
    ia, ka, core = lax.axis_index("ia"), lax.axis_index("ka"), lax.axis_index("ja") % 2
    low_lanes = iota((RANK, LANES), 1) < 64
    even = jnp.where(core == 0, mine_ref[...], other_ref[...])
    odd = jnp.where(core == 0, other_ref[...], mine_ref[...])
    parts = []
    for p in range(2):
        one, two = even[:, 128 * p : 128 * p + 128], odd[:, 128 * p : 128 * p + 128]
        parts.append(jnp.where(low_lanes, one, pltpu.roll(two, 64, 1)))
        parts.append(jnp.where(low_lanes, pltpu.roll(one, 64, 1), two))
    m = jnp.concatenate(parts, axis=1)
    a = jnp.dot(inv_ref[...], m, precision=HIGH, preferred_element_type=F32)
    for q in range(4):
        pair = a[:, 128 * q : 128 * q + 128]
        scratch[2 * q] = pair
        scratch[2 * q + 1] = pltpu.roll(pair, 64, 1)
    a_ref[...] = scratch[ka]
    gram = folded_gram(a)
    c = c_ref[...]
    highs, lows = [], []
    for k in range(8):
        high, low = split(a * c[:, k : k + 1])
        highs.append(high)
        lows.append(low)
    left = jnp.concatenate([jnp.concatenate(highs, axis=1), jnp.concatenate(lows, axis=1)], axis=0)
    both = jnp.dot(left, t_ref[...].reshape(4096, 512), preferred_element_type=F32)
    out = both[:RANK] + both[RANK:]
    for q in range(4):
        quarters[q] = out[:, 128 * q : 128 * q + 128]
    for n, ref in enumerate((p0_ref, p1_ref, p2_ref, p3_ref)):
        ref[:RANK] = quarters[(ia + n) % 4]
        ref[RANK:] = gram


def sum_kernel(p0_ref, p1_ref, p2_ref, p3_ref, u_ref, gram_ref):
    p = (p0_ref[...] + p1_ref[...]) + (p2_ref[...] + p3_ref[...])
    for n in range(8):
        u_ref[n] = p[:RANK]
    gram_ref[...] = p[RANK:]


def second_solve_kernel(total_i, u_ref, gram_ref, gram_c_ref, ss_ref, scale_ref):
    half = lax.axis_index("ka") % 2
    gram = unfold(gram_ref[...])
    diag = jnp.where(iota(gram.shape, 0) == iota(gram.shape, 1), gram, 0.0)
    scale_col = lax.rsqrt(jnp.sum(diag, axis=1, keepdims=True) / total_i + EPS)
    scale_row = lax.rsqrt(jnp.sum(diag, axis=0, keepdims=True) / total_i + EPS)
    inv = inverse(gram * scale_col * scale_row * gram_c_ref[...])
    scale_ref[...] = jnp.broadcast_to(scale_col, (RANK, LANES))
    m = total(u_ref) * scale_col
    raw = jnp.dot(inv, m, precision=HIGH, preferred_element_type=F32)
    ss = jnp.sum(raw * raw, axis=1, keepdims=True)
    place = iota((RANK, LANES), 0) == iota((RANK, LANES), 1)
    ss_row = jnp.sum(jnp.where(place, ss, 0.0), axis=0, keepdims=True)
    raw = jnp.where(half == 0, raw, pltpu.roll(raw, 64, 1))
    turned_raw = pltpu.roll(raw, 64, 1)
    low_lanes = iota((4, LANES), 1) < 64
    for ia in range(4):
        data = jnp.where(low_lanes, raw[8 * ia : 8 * ia + 4], turned_raw[8 * ia + 4 : 8 * ia + 8])
        tile = jnp.concatenate([data, ss_row], axis=0)
        for ja in range(8):
            start = 5 * (8 * ia + ja)
            ss_ref[start : start + 5] = tile


def finish_kernel(total_j, ss_ref, a_ref, scale_ref, out_a_ref, out_b_ref):
    ia, ja, ka = lax.axis_index("ia"), lax.axis_index("ja"), lax.axis_index("ka")
    place = iota((8, LANES), 1) == iota((8, LANES), 0) + 8 * ia
    ss_row = jnp.sum(ss_ref[pl.ds(4, 32, stride=5), :], axis=0, keepdims=True)
    ss = jnp.sum(jnp.where(place, ss_row, 0.0), axis=1, keepdims=True)
    data = ss_ref[pl.ds(5 * (8 * (ka // 2) + ja), 4), :]
    b = jnp.concatenate([data, pltpu.roll(data, 64, 1)], axis=0) * lax.rsqrt(ss / total_j + EPS)
    out_b_ref[...] = b[:, :64]
    out_a_ref[...] = pltpu.roll(a_ref[...] * scale_ref[...], (32 - 4 * ja) % 32, 0)[:4, :64]


def call(kernel, outs, *args, scratch=(), cost=None, space=VMEM):
    return pl.pallas_call(
        kernel,
        out_shape=[jax.ShapeDtypeStruct(s, F32) for s in outs],
        in_specs=[space] * len(args),
        out_specs=[VMEM] * len(outs),
        scratch_shapes=scratch,
        cost_estimate=cost,
        compiler_params=pltpu.CompilerParams(vmem_limit_bytes=32 * 1024 * 1024),
    )(*args)


def exchange(x, axes, groups=None):
    return lax.all_to_all(x, axes, 0, 0, tiled=True, axis_index_groups=groups)


def other_core(x):
    return lax.ppermute(x, "ja", [(n, n ^ 1) for n in range(8)])


def turned(x, axis, step):
    size = lax.axis_size(axis)
    return lax.ppermute(x, axis, [(n, (n + step) % size) for n in range(size)])


def body(tensor, factor_b, factor_c):
    total_i = tensor.shape[1] * lax.axis_size("ia")
    total_j = tensor.shape[2] * lax.axis_size("ja")
    factor_b, factor_c = (
        pltpu.with_memory_space_constraint(a, pltpu.HBM) for a in (factor_b, factor_c)
    )
    (y,) = call(
        start_kernel,
        [(160, LANES)],
        factor_b,
        factor_c,
        scratch=[
            pltpu.VMEM(factor_b.shape, F32),
            pltpu.VMEM(factor_c.shape, F32),
            pltpu.SemaphoreType.DMA((2,)),
        ],
        cost=LONG,
        space=HBM,
    )
    y = exchange(y.reshape(32, 1, 5 * LANES), ("ia", "ka")).reshape(160, LANES)
    half = (4, 144, LANES)
    send, extra = call(
        lambda *refs: first_kernel(True, *refs), [half, (16, LANES)], y, tensor
    )
    received = other_core(send)
    (keep,) = call(lambda *refs: first_kernel(False, *refs), [half], y, tensor, extra)
    z = [keep[n] + received[n] for n in range(4)]
    z = [z[0]] + [turned(z[n], "ja", 2 * n) for n in range(1, 4)]
    same_core = [[8 * ja + ka for ja in range(core, 8, 2) for ka in range(8)] for core in range(2)]
    u, gram_b, c_all, c_here = call(
        combine_kernel,
        [(32, 16, LANES), (RANK, RANK), (RANK, 64), (RANK, LANES)],
        *z,
        scratch=[pltpu.VMEM((RANK, LANES), F32)],
    )
    v = exchange(u, ("ja", "ka"), same_core)
    (m,) = call(turn_kernel, [(RANK, 256)], v, cost=LONG)
    inv_a, gram_c = call(invert_a_kernel, [(RANK, RANK), (RANK, RANK)], gram_b, c_all)
    *p, a = call(
        second_kernel,
        [(40, LANES)] * 4 + [(RANK, LANES)],
        m,
        other_core(m),
        inv_a,
        tensor,
        c_here,
        scratch=[pltpu.VMEM((8, RANK, LANES), F32), pltpu.VMEM((4, RANK, LANES), F32)],
    )
    p = [p[0]] + [turned(p[n], "ia", n) for n in range(1, 4)]
    u, gram_a = call(sum_kernel, [(8, RANK, LANES), (8, LANES)], *p)
    u = exchange(u, "ka")
    ss, scale_a = call(
        lambda *refs: second_solve_kernel(total_i, *refs),
        [(160, LANES), (RANK, LANES)],
        u,
        gram_a,
        gram_c,
    )
    ss = exchange(ss.reshape(32, 1, 5 * LANES), ("ia", "ja")).reshape(160, LANES)
    out_a, out_b = call(
        lambda *refs: finish_kernel(total_j, *refs), [(4, 64), (8, 64)], ss, a, scale_a
    )
    return out_a, out_b


def solution(mesh):
    return jax.shard_map(
        body,
        mesh=mesh,
        in_specs=(P("ka", "ia", "ja"), P("ia", ("ja", "ka")), P(("ia", "ja"), "ka")),
        out_specs=(P("ja", ("ia", "ka")), P("ia", ("ja", "ka"))),
        check_vma=False,
    )
```
